32 devices in a mesh: row: 4 (over x, core), col: 8 (over z, y).
Axes of the slice: x: 2, y: 2, z: 4, core: 2. Of those that a mesh axis runs over, the one named last changes fastest.
Arguments:
- volt_init: float32 [32, 128, 400], P('row', 'col'), may hold values from -6 to 6
- curr_init: float32 [32, 128, 400], P('row', 'col'), may hold values from -6 to 6
- local_inverse: bfloat16 [32, 400, 400], P('row'), may hold values from -1 to 2, as said below
- schur_inverse: bfloat16 [4096, 4096], P('row', 'col'), may hold values from -1 to 2, as said below
- ind_gain: float32 [32, 400], P('row'), may hold values from 0.05 to 0.5
- tie: float32 [32, 64], P('row'), may hold values from 0.3 to 3
- port_map: int32 [32, 64], P('row'), may hold values from 0 to 4095
- breaker: int32 [32, 128, 400], P('row', 'col'), may hold values 0 or 1
- fault_time: int32 [128], P('col'), may hold values from 0 to 2
- fault_node: int32 [128], P('col'), may hold values from 0 to 12799
Outputs:
- volt_final: float32 [32, 128, 400], P('row', 'col')
- curr_final: float32 [32, 128, 400], P('row', 'col')
- iface_volt: float32 [128, 4096], P('col', 'row')
The draws below stay inside these ranges and needn't reach their ends.
Inputs may be any that keep to these rules, and one draw needn't show every extreme that they name: `local_inverse`: diagonal entries between 0.5 and 1.5; off-diagonal entries independent. `schur_inverse`: diagonal entries between 0.5 and 1.5; off-diagonal entries independent.
All inputs are finite; a program needn't handle non-finite values. No bound on the sum of `breaker` on one device may be relied on, other than what follows from the above.
Results may differ from the reference program's by a relative error of at most 0.0068.
Values may be sent and summed in bfloat16 or wider, within the bound.
A program may use at most 64 MiB of HBM per device.

```python
import math
import jax
import jax.numpy as jnp
from jax import lax

NODES = 400
PORTS = 64
NI = 4096
STEPS = 2
SUBNETS = 32
SCEN = 128


def dominant(key, count, order):
    first, second = jax.random.split(key)
    diag = jax.random.uniform(first, (count, order), jnp.float32, 0.5, 1.5)
    return (diag, second)


def draw_local_inverse(key, part):
    key = jax.random.fold_in(key, 11)
    diag, second = dominant(key, SUBNETS, NODES)
    shape = (SUBNETS, NODES, NODES)
    off_diag = jnp.clip(jax.random.normal(second, shape, jnp.float32), -5.0, 5.0)
    off_diag = off_diag * (0.6 / math.sqrt(NODES))
    rows = lax.broadcasted_iota(jnp.int32, shape, 1)
    cols = lax.broadcasted_iota(jnp.int32, shape, 2)
    full = jnp.where(rows == cols, diag[:, :, None], off_diag)
    return full.astype(jnp.bfloat16)


def draw_schur_inverse(key, part):
    key = jax.random.fold_in(key, 12)
    diag, second = dominant(key, 1, NI)
    shape = (NI, NI)
    off_diag = jnp.clip(jax.random.normal(second, shape, jnp.float32), -5.0, 5.0)
    off_diag = off_diag * (0.6 / math.sqrt(NI))
    rows = lax.broadcasted_iota(jnp.int32, shape, 0)
    cols = lax.broadcasted_iota(jnp.int32, shape, 1)
    full = jnp.where(rows == cols, diag[0][:, None], off_diag)
    return full.astype(jnp.bfloat16)


def set_ends(values, stream_key, low, largest):
    place = [jax.random.randint(jax.random.fold_in(stream_key, axis), (), 0, length) for axis, length in enumerate(values.shape)]
    longest = values.shape.index(max(values.shape))
    next_to = place[:longest] + [(place[longest] + 1) % values.shape[longest]] + place[longest + 1:]
    return values.at[tuple(place)].set(low).at[tuple(next_to)].set(largest)


def steps_of(rng, dims, cuts, low, top_value):
    loudness = 1.0
    for position, shards_of in cuts:
        draws = jax.random.uniform(jax.random.fold_in(jax.random.fold_in(rng, 6), position), (shards_of,), jnp.float32, low / len(cuts), top_value / len(cuts))
        loudness = loudness * jnp.repeat(jnp.exp(draws), dims[position] // shards_of).reshape((-1,) + (1,) * (len(dims) - 1 - position))
    return loudness


def bell_draw(key, dims, width, bound, cuts=(), kind=jnp.bfloat16):
    level = steps_of(key, dims, cuts, -0.22, 0.18) if cuts else 1.0
    values = jax.random.normal(key, dims, jnp.float32) * width * level
    return jnp.minimum(jnp.maximum(values, -bound), bound).astype(kind)


def setup_inputs(seed: int = 0) -> dict:
    key_of = jax.random.split(jax.random.key(seed), 11)
    volt_init = bell_draw(key_of[0], (SUBNETS, SCEN, NODES), 1.0, 6.0, ((0, 4), (1, 8)), jnp.float32)
    curr_init = bell_draw(key_of[1], (SUBNETS, SCEN, NODES), 1.0, 6.0, ((0, 4), (1, 8)), jnp.float32)
    local_inverse = draw_local_inverse(jax.random.fold_in(key_of[10], 71), 0)
    schur_inverse = draw_schur_inverse(jax.random.fold_in(key_of[10], 71), 0)
    ind_gain = jnp.clip(jnp.exp(math.log(0.5) - 2.3025851 * jax.random.uniform(key_of[4], (SUBNETS, NODES), jnp.float32) ** steps_of(key_of[4], (SUBNETS, NODES), ((0, 4),), -0.2, 0.2)), 0.05, 0.5)
    tie = jnp.clip(jnp.exp(math.log(3.0) - 2.3025851 * jax.random.uniform(key_of[5], (SUBNETS, PORTS), jnp.float32) ** steps_of(key_of[5], (SUBNETS, PORTS), ((0, 4),), -0.2, 0.2)), 0.3, 3.0)
    port_map = set_ends(jax.random.randint(key_of[6], (SUBNETS, PORTS), 0, NI), jax.random.fold_in(key_of[6], 1), 0, NI - 1).astype(jnp.int32)
    breaker = set_ends((jax.random.randint(key_of[7], (SUBNETS, SCEN, NODES), 0, 8) < 7).astype(jnp.int32), jax.random.fold_in(key_of[7], 1), 0, 1)
    fault_time = set_ends(jax.random.randint(key_of[8], (SCEN,), 0, STEPS + 1), jax.random.fold_in(key_of[8], 1), 0, STEPS).astype(jnp.int32)
    fault_node = set_ends(jax.random.randint(key_of[9], (SCEN,), 0, SUBNETS * NODES), jax.random.fold_in(key_of[9], 1), 0, (SUBNETS * NODES) - 1).astype(jnp.int32)
    return {"volt_init": volt_init, "curr_init": curr_init, "local_inverse": local_inverse, "schur_inverse": schur_inverse, "ind_gain": ind_gain, "tie": tie, "port_map": port_map, "breaker": breaker, "fault_time": fault_time, "fault_node": fault_node}


def reference(volt_init, curr_init, local_inverse, schur_inverse, ind_gain, tie, port_map, breaker, fault_time, fault_node):
    volt = volt_init
    curr = curr_init
    closed = breaker.astype(jnp.float32)
    inverse_wide = local_inverse.astype(jnp.float32)
    schur_wide = schur_inverse.astype(jnp.float32)
    node_ids = (jnp.arange(SUBNETS, dtype=jnp.int32)[:, None] * NODES + jnp.arange(NODES, dtype=jnp.int32)[None, :])
    hits = (node_ids[:, None, :] == fault_node[None, :, None])
    flat_map = port_map.reshape(-1)
    iface_volt = jnp.zeros((SCEN, NI), jnp.float32)
    for step in range(STEPS):
        hist = closed * (curr + ind_gain[:, None, :] * volt)
        active = (step >= fault_time)[None, :, None]
        fault_on = jnp.where(hits & active, 1.0, 0.0).astype(jnp.float32)
        inject = (-hist - 2.0 * fault_on * volt).astype(jnp.bfloat16)
        open_volt = jnp.einsum("ksn,knm->ksm", inject.astype(jnp.float32), inverse_wide, precision=lax.Precision.HIGHEST)
        values = tie[:, None, :] * open_volt[:, :, :PORTS]
        flat_values = jnp.transpose(values, (0, 2, 1)).reshape(SUBNETS * PORTS, SCEN)
        iface_rhs = jax.ops.segment_sum(flat_values, flat_map, NI).T
        rhs_half = iface_rhs.astype(jnp.bfloat16)
        iface_volt = lax.dot_general(rhs_half.astype(jnp.float32), schur_wide, (((1,), (1,)), ((), ())), precision=lax.Precision.HIGHEST)
        picked = jnp.take(iface_volt, flat_map, axis=1).reshape(SCEN, SUBNETS, PORTS)
        drive = (tie[:, None, :] * jnp.transpose(picked, (1, 0, 2))).astype(jnp.bfloat16)
        volt_next = open_volt + jnp.einsum("ksp,kpn->ksn", drive.astype(jnp.float32), inverse_wide[:, :PORTS, :], precision=lax.Precision.HIGHEST)
        curr = closed * (curr + ind_gain[:, None, :] * (volt_next + volt))
        volt = volt_next
    return volt, curr, iface_volt
```

```python
import functools

import jax
import jax.numpy as jnp
from jax import lax
from jax.experimental import pallas as pl
from jax.experimental.pallas import tpu as pltpu
from jax.sharding import PartitionSpec as P

STEPS = 2
LANES = 128
MESH = pl.DeviceIdType.MESH
F32 = jnp.float32
BF16 = jnp.bfloat16


def halves(x):
    high = x.astype(BF16)
    low = (x - high.astype(F32)).astype(BF16)
    return jnp.concatenate([high, low], axis=0)


def joined(x, count):
    return x[:count].astype(F32) + x[count:].astype(F32)


def dot_nt(a, b):
    return lax.dot_general(a, b, (((1,), (1,)), ((), ())), preferred_element_type=F32)


def dot_nn(a, b):
    return lax.dot_general(a, b, (((1,), (0,)), ((), ())), preferred_element_type=F32)


def kernel(
    rows,
    cols,
    volt_ref,
    curr_ref,
    linv_hbm,
    schur_hbm,
    gain_ref,
    tie_ref,
    map_ref,
    breaker_ref,
    time_ref,
    node_ref,
    volt_out,
    curr_out,
    iface_out,
    linv,
    schur,
    open_volt,
    map_in,
    spread,
    pick,
    val_in,
    rhs_send,
    rhs_in,
    part_send,
    part_in,
    pick_send,
    pick_in,
    load_sem,
    send_sem,
    recv_sem,
):
    sub, scen, nodes = volt_ref.shape
    ports = tie_ref.shape[1]
    half = sub // 2
    own_i, own_j = schur.shape
    share = own_j // rows
    r = lax.axis_index("row")
    c = lax.axis_index("col")
    others = rows * cols - 1

    load_linv = pltpu.make_async_copy(linv_hbm, linv, load_sem.at[0])
    load_schur = pltpu.make_async_copy(schur_hbm, schur, load_sem.at[1])
    load_linv.start()
    load_schur.start()

    barrier = pltpu.get_barrier_semaphore()

    def greet(t, _):
        there = (lax.rem(r + t // cols, rows), lax.rem(c + lax.rem(t, cols), cols))
        pl.semaphore_signal(barrier, inc=1, device_id=there, device_id_type=MESH)
        return 0

    lax.fori_loop(1, rows * cols, greet, 0)

    def wait_bytes(ref, sem):
        pltpu.make_async_copy(ref, ref, sem).wait()

    def send(src, dst, phase, there):
        pltpu.make_async_remote_copy(
            src_ref=src,
            dst_ref=dst,
            send_sem=send_sem.at[phase],
            recv_sem=recv_sem.at[phase],
            device_id=there,
            device_id_type=MESH,
        ).start()

    def send_row(src_of, dst, phase):
        for d in range(1, rows):
            peer = lax.rem(r + d, rows)
            send(src_of(peer), dst, phase, (peer, c))

    scen_ids = lax.broadcasted_iota(jnp.int32, (scen, 1), 0)
    f_node = jnp.zeros((scen, 1), jnp.int32)
    f_time = jnp.zeros((scen, 1), jnp.int32)
    for s in range(scen):
        f_node = jnp.where(scen_ids == s, node_ref[s], f_node)
        f_time = jnp.where(scen_ids == s, time_ref[s], f_time)
    node_ids = lax.broadcasted_iota(jnp.int32, (scen, nodes), 1)

    def injection(step, k, volt, curr):
        closed = breaker_ref[k].astype(F32)
        hist = closed * (curr + gain_ref[k : k + 1, :] * volt)
        here = f_node - (r * sub + k) * nodes
        on = jnp.logical_and(node_ids == here, f_time <= step)
        fault_on = jnp.where(on, 1.0, 0.0).astype(F32)
        return (-hist - 2.0 * fault_on * volt).astype(BF16)

    def port_values(k):
        return tie_ref[k : k + 1, :] * open_volt[k, :, :ports]

    pl.semaphore_wait(barrier, others)
    send_row(lambda peer: map_ref, map_in.at[r], 0)
    map_in[r] = map_ref[...]
    load_linv.wait()

    for step in range(STEPS):
        base = 1 + 4 * step
        for k in range(sub):
            if step == 0:
                inject = injection(step, k, volt_ref[k], curr_ref[k])
            else:
                inject = injection(step, k, volt_out[k], curr_out[k])
            open_volt[k] = dot_nn(inject, linv[k])
        vals = jnp.concatenate(
            [
                jnp.concatenate([port_values(g), port_values(g + half)], axis=1)
                for g in range(half)
            ],
            axis=1,
        )
        val_in[step, r] = halves(vals)
        send_row(lambda peer: val_in.at[step, r], val_in.at[step, r], base)

        if step == 0:
            wait_bytes(map_in.at[pl.ds(0, rows - 1)], recv_sem.at[0])
            wait_bytes(map_in.at[pl.ds(0, rows - 1)], send_sem.at[0])
            ids = lax.broadcasted_iota(jnp.int32, (share, LANES), 0)

            def packed_map(q, g):
                m = map_in[q]
                return jnp.concatenate([m[g : g + 1], m[g + half : g + half + 1]], axis=1)

            def fill_spread(q, _):
                for g in range(half):
                    m = packed_map(q, g)
                    for b in range(cols):
                        hit = ids == m - (b * own_j + r * share)
                        spread[q, b * share : (b + 1) * share, g * LANES : (g + 1) * LANES] = (
                            jnp.where(hit, 1.0, 0.0).astype(BF16)
                        )
                return 0

            lax.fori_loop(0, rows, fill_spread, 0)

        wait_bytes(val_in.at[step, pl.ds(0, rows - 1)], recv_sem.at[base])
        rhs = dot_nt(val_in[step, 0], spread[0])
        for q in range(1, rows):
            rhs += dot_nt(val_in[step, q], spread[q])
        rhs = joined(rhs, scen).astype(BF16)
        for b in range(cols):
            rhs_send[step, b] = rhs[:, b * share : (b + 1) * share]

        def send_rhs(t, _):
            peer_r = lax.rem(r + t // cols, rows)
            peer_c = lax.rem(c + lax.rem(t, cols), cols)
            send(
                rhs_send.at[step, peer_c],
                rhs_in.at[step, r * cols + c],
                base + 1,
                (peer_r, peer_c),
            )
            return 0

        lax.fori_loop(1, rows * cols, send_rhs, 0)
        rhs_in[step, r * cols + c] = rhs_send[step, c]

        if step == 0:
            load_schur.wait()
            pick_ids = lax.broadcasted_iota(jnp.int32, (own_i, LANES), 0)

            def fill_pick(q, _):
                for g in range(half):
                    m = packed_map(q, g) - r * own_i
                    pick[q, :, g * LANES : (g + 1) * LANES] = jnp.where(
                        pick_ids == m, 1.0, 0.0
                    ).astype(BF16)
                return 0

            lax.fori_loop(0, rows, fill_pick, 0)

        wait_bytes(rhs_in.at[step, pl.ds(0, others)], recv_sem.at[base + 1])
        wide = jnp.concatenate(
            [
                rhs_in[step, q * cols : (q + 1) * cols].reshape(cols * scen, share)
                for q in range(rows)
            ],
            axis=1,
        )
        part = dot_nt(wide, schur[...]).astype(BF16)
        part_send[step] = part.reshape(cols, scen, own_i)
        for d in range(1, cols):
            peer = lax.rem(c + d, cols)
            send(part_send.at[step, peer], part_in.at[step, c], base + 2, (r, peer))
        part_in[step, c] = part_send[step, c]

        wait_bytes(part_in.at[step, pl.ds(0, cols - 1)], recv_sem.at[base + 2])
        iface = part_in[step, 0].astype(F32)
        for b in range(1, cols):
            iface += part_in[step, b].astype(F32)
        if step == STEPS - 1:
            iface_out[...] = iface
        iface_halves = halves(iface)
        for q in range(rows):
            pick_send[step, q] = dot_nn(iface_halves, pick[q]).astype(BF16)
        send_row(lambda peer: pick_send.at[step, peer], pick_in.at[step, r], base + 3)
        pick_in[step, r] = pick_send[step, r]
        wait_bytes(pick_in.at[step, pl.ds(0, rows - 1)], recv_sem.at[base + 3])
        picked = joined(pick_in[step, 0], scen)
        for q in range(1, rows):
            picked += joined(pick_in[step, q], scen)

        for k in range(sub):
            first = (k % half) * LANES + (k // half) * ports
            drive = (tie_ref[k : k + 1, :] * picked[:, first : first + ports]).astype(BF16)
            volt_next = open_volt[k] + dot_nn(drive, linv[k, :ports, :])
            if step == 0:
                volt, curr = volt_ref[k], curr_ref[k]
            else:
                volt, curr = volt_out[k], curr_out[k]
            closed = breaker_ref[k].astype(F32)
            curr_out[k] = closed * (curr + gain_ref[k : k + 1, :] * (volt_next + volt))
            volt_out[k] = volt_next

        wait_bytes(val_in.at[step, pl.ds(0, rows - 1)], send_sem.at[base])
        wait_bytes(rhs_in.at[step, pl.ds(0, others)], send_sem.at[base + 1])
        wait_bytes(part_in.at[step, pl.ds(0, cols - 1)], send_sem.at[base + 2])
        wait_bytes(pick_in.at[step, pl.ds(0, rows - 1)], send_sem.at[base + 3])


def fused(
    volt_init,
    curr_init,
    local_inverse,
    schur_inverse,
    ind_gain,
    tie,
    port_map,
    breaker,
    fault_time,
    fault_node,
):
    rows, cols = lax.axis_size("row"), lax.axis_size("col")
    sub, scen, nodes = volt_init.shape
    ports = tie.shape[1]
    own_i, own_j = schur_inverse.shape
    share = own_j // rows
    flat = sub * ports
    vmem = pl.BlockSpec(memory_space=pltpu.VMEM)
    smem = pl.BlockSpec(memory_space=pltpu.SMEM)
    anywhere = pl.BlockSpec(memory_space=pl.ANY)
    return pl.pallas_call(
        functools.partial(kernel, rows, cols),
        out_shape=(
            jax.ShapeDtypeStruct(volt_init.shape, F32),
            jax.ShapeDtypeStruct(volt_init.shape, F32),
            jax.ShapeDtypeStruct((scen, own_i), F32),
        ),
        in_specs=[vmem, vmem, anywhere, anywhere, vmem, vmem, vmem, vmem, smem, smem],
        out_specs=(vmem, vmem, vmem),
        scratch_shapes=[
            pltpu.VMEM(local_inverse.shape, BF16),
            pltpu.VMEM(schur_inverse.shape, BF16),
            pltpu.VMEM(volt_init.shape, F32),
            pltpu.VMEM((rows, sub, ports), jnp.int32),
            pltpu.VMEM((rows, cols * share, flat), BF16),
            pltpu.VMEM((rows, own_i, flat), BF16),
            pltpu.VMEM((STEPS, rows, 2 * scen, flat), BF16),
            pltpu.VMEM((STEPS, cols, scen, share), BF16),
            pltpu.VMEM((STEPS, rows * cols, scen, share), BF16),
            pltpu.VMEM((STEPS, cols, scen, own_i), BF16),
            pltpu.VMEM((STEPS, cols, scen, own_i), BF16),
            pltpu.VMEM((STEPS, rows, 2 * scen, flat), BF16),
            pltpu.VMEM((STEPS, rows, 2 * scen, flat), BF16),
            pltpu.SemaphoreType.DMA((2,)),
            pltpu.SemaphoreType.DMA((1 + 4 * STEPS,)),
            pltpu.SemaphoreType.DMA((1 + 4 * STEPS,)),
        ],
        compiler_params=pltpu.CompilerParams(
            collective_id=0, has_side_effects=True, vmem_limit_bytes=48 * 1024 * 1024
        ),
    )(
        volt_init,
        curr_init,
        local_inverse,
        schur_inverse,
        ind_gain,
        tie,
        port_map,
        breaker,
        fault_time,
        fault_node,
    )


def plain(
    volt_init,
    curr_init,
    local_inverse,
    schur_inverse,
    ind_gain,
    tie,
    port_map,
    breaker,
    fault_time,
    fault_node,
):
    sub_count, scen_count, node_count = volt_init.shape
    port_count = tie.shape[1]
    iface_width = lax.axis_size("row") * schur_inverse.shape[0]
    volt = volt_init
    curr = curr_init
    closed = breaker.astype(F32)
    first_sub = lax.axis_index("row") * sub_count
    node_ids = (first_sub + jnp.arange(sub_count, dtype=jnp.int32))[
        :, None
    ] * node_count + jnp.arange(node_count, dtype=jnp.int32)[None, :]
    hits = node_ids[:, None, :] == fault_node[None, :, None]
    flat_map = port_map.reshape(-1)
    port_inverse = local_inverse[:, :port_count, :]
    iface_block = jnp.zeros((scen_count, schur_inverse.shape[0]), F32)
    for step in range(STEPS):
        hist = closed * (curr + ind_gain[:, None, :] * volt)
        active = (step >= fault_time)[None, :, None]
        fault_on = jnp.where(hits & active, 1.0, 0.0).astype(F32)
        inject = (-hist - 2.0 * fault_on * volt).astype(BF16)
        open_volt = jnp.einsum("ksn,knm->ksm", inject, local_inverse, preferred_element_type=F32)
        values = tie[:, None, :] * open_volt[:, :, :port_count]
        flat_values = jnp.transpose(values, (0, 2, 1)).reshape(sub_count * port_count, scen_count)
        partial_rhs = jax.ops.segment_sum(flat_values, flat_map, iface_width).T
        owned = lax.psum_scatter(partial_rhs, "row", scatter_dimension=1, tiled=True)
        rhs_half = lax.all_gather(owned.astype(BF16), "row", axis=1, tiled=True)
        iface_block = dot_nt(rhs_half, lax.all_gather(schur_inverse, "col", axis=1, tiled=True))
        iface_full = lax.all_gather(iface_block, "row", axis=1, tiled=True)
        picked = jnp.take(iface_full, flat_map, axis=1).reshape(scen_count, sub_count, port_count)
        drive = (tie[:, None, :] * jnp.transpose(picked, (1, 0, 2))).astype(BF16)
        volt_next = open_volt + jnp.einsum(
            "ksp,kpn->ksn", drive, port_inverse, preferred_element_type=F32
        )
        curr = closed * (curr + ind_gain[:, None, :] * (volt_next + volt))
        volt = volt_next
    return (volt, curr, iface_block)


def local(*args):
    volt_init, schur_inverse, tie = args[0], args[3], args[5]
    sub, scen, _ = volt_init.shape
    own_i, own_j = schur_inverse.shape
    aligned = (
        own_j % (lax.axis_size("row") * LANES) == 0
        and own_i % LANES == 0
        and scen % 16 == 0
        and sub % 2 == 0
        and 2 * tie.shape[1] == LANES
    )
    return fused(*args) if aligned else plain(*args)


def solution(mesh):
    placed = (
        P("row", "col", None),
        P("row", "col", None),
        P("row", None, None),
        P("row", "col"),
        P("row", None),
        P("row", None),
        P("row", None),
        P("row", "col", None),
        P("col"),
        P("col"),
    )
    return jax.shard_map(
        local,
        mesh=mesh,
        in_specs=placed,
        out_specs=(P("row", "col", None), P("row", "col", None), P("col", "row")),
        check_vma=False,
    )
```

```python
import functools

import jax
import jax.numpy as jnp
from jax import lax
from jax.experimental import pallas as pl
from jax.experimental.pallas import tpu as pltpu
from jax.sharding import PartitionSpec as P

STEPS = 2
PIECES = 2
LANES = 128
MESH = pl.DeviceIdType.MESH
F32 = jnp.float32
BF16 = jnp.bfloat16


def halves(x):
    high = x.astype(BF16)
    low = (x - high.astype(F32)).astype(BF16)
    return jnp.concatenate([high, low], axis=0)


def joined(x, count):
    return x[:count].astype(F32) + x[count:].astype(F32)


def dot_nt(a, b):
    return lax.dot_general(a, b, (((1,), (1,)), ((), ())), preferred_element_type=F32)


def dot_nn(a, b):
    return lax.dot_general(a, b, (((1,), (0,)), ((), ())), preferred_element_type=F32)


def kernel(
    rows,
    cols,
    volt_hbm,
    curr_hbm,
    linv_hbm,
    schur_hbm,
    gain_hbm,
    tie_hbm,
    map_hbm,
    breaker_hbm,
    time_hbm,
    node_hbm,
    volt_out,
    curr_out,
    iface_out,
    volt_ref,
    curr_ref,
    linv,
    schur,
    gain_ref,
    tie_ref,
    map_ref,
    breaker_ref,
    time_ref,
    node_ref,
    open_volt,
    map_in,
    spread,
    pick,
    val_in,
    rhs_send,
    rhs_in,
    part_send,
    part_in,
    pick_send,
    pick_in,
    load_sem,
    send_sem,
    recv_sem,
    val_sem,
):
    sub, scen, nodes = volt_ref.shape
    ports = tie_ref.shape[1]
    half = sub // 2
    own_i, own_j = schur.shape
    share = own_j // rows
    piece = own_i // PIECES
    r = lax.axis_index("row")
    c = lax.axis_index("col")
    others = rows * cols - 1

    loads = [
        pltpu.make_async_copy(src, dst, load_sem.at[n])
        for n, (src, dst) in enumerate(
            (
                (time_hbm, time_ref),
                (node_hbm, node_ref),
                (gain_hbm, gain_ref),
                (tie_hbm, tie_ref),
                (map_hbm, map_ref),
                (volt_hbm, volt_ref),
                (curr_hbm, curr_ref),
                (breaker_hbm, breaker_ref),
                (linv_hbm, linv),
                (schur_hbm, schur),
            )
        )
    ]
    for load in loads:
        load.start()

    barrier = pltpu.get_barrier_semaphore()

    def greet(t, _):
        there = (lax.rem(r + t // cols, rows), lax.rem(c + lax.rem(t, cols), cols))
        pl.semaphore_signal(barrier, inc=1, device_id=there, device_id_type=MESH)
        return 0

    lax.fori_loop(1, rows * cols, greet, 0)
    for load in loads[:-1]:
        load.wait()

    def wait_bytes(ref, sem):
        pltpu.make_async_copy(ref, ref, sem).wait()

    def send(src, dst, phase, there, recv=None):
        pltpu.make_async_remote_copy(
            src_ref=src,
            dst_ref=dst,
            send_sem=send_sem.at[phase],
            recv_sem=recv_sem.at[phase] if recv is None else recv,
            device_id=there,
            device_id_type=MESH,
        ).start()

    def row_peer(d):
        return lax.rem(r + d, rows)

    far_first = sorted(range(1, rows), key=lambda d: abs(d - rows // 2))

    scen_ids = lax.broadcasted_iota(jnp.int32, (scen, 1), 0)
    f_node = jnp.zeros((scen, 1), jnp.int32)
    f_time = jnp.zeros((scen, 1), jnp.int32)
    for s in range(scen):
        f_node = jnp.where(scen_ids == s, node_ref[s], f_node)
        f_time = jnp.where(scen_ids == s, time_ref[s], f_time)
    node_ids = lax.broadcasted_iota(jnp.int32, (scen, nodes), 1)

    def injection(step, k, volt, curr):
        closed = breaker_ref[k].astype(F32)
        hist = closed * (curr + gain_ref[k : k + 1, :] * volt)
        here = f_node - (r * sub + k) * nodes
        on = jnp.logical_and(node_ids == here, f_time <= step)
        fault_on = jnp.where(on, 1.0, 0.0).astype(F32)
        return (-hist - 2.0 * fault_on * volt).astype(BF16)

    ids = lax.broadcasted_iota(jnp.int32, (LANES, LANES), 0).astype(F32).astype(BF16)
    one = jnp.ones((LANES, LANES), BF16)
    zero = jnp.zeros((LANES, LANES), BF16)

    def hits(m):
        near = jnp.clip(m, -1, LANES).astype(F32).astype(BF16)
        return jnp.where(ids == near, one, zero)

    def packed_map(m, g):
        return jnp.concatenate([m[g : g + 1], m[g + half : g + half + 1]], axis=1)

    def fill_spread(q, maps):
        for g in range(half):
            m = packed_map(maps, g)
            for b in range(cols):
                for e in range(share // LANES):
                    first = b * share + e * LANES
                    spread[q, first : first + LANES, g * LANES : (g + 1) * LANES] = hits(
                        m - (b * own_j + r * share + e * LANES)
                    )

    def fill_pick(q, maps):
        for g in range(half):
            m = packed_map(maps, g) - r * own_i
            for e in range(own_i // LANES):
                pick[q, e * LANES : (e + 1) * LANES, g * LANES : (g + 1) * LANES] = hits(
                    m - e * LANES
                )

    for step in range(STEPS):
        base = 1 + (3 + PIECES) * step
        volt_now, curr_now = (volt_ref, curr_ref) if step == 0 else (volt_out, curr_out)
        injects = [injection(step, k, volt_now[k], curr_now[k]) for k in range(sub)]
        for k in range(sub):
            open_volt[k] = dot_nn(injects[k], linv[k])

        def port_values(k):
            return tie_ref[k : k + 1, :] * open_volt[k, :, :ports]

        vals = jnp.concatenate(
            [
                jnp.concatenate([port_values(g), port_values(g + half)], axis=1)
                for g in range(half)
            ],
            axis=1,
        )
        val_in[step, r] = halves(vals)
        if step == 0:
            pl.semaphore_wait(barrier, others)
            for d in far_first:
                send(map_ref, map_in.at[r], 0, (row_peer(d), c))
        for d in far_first:
            mine = val_in.at[step, r]
            send(mine, mine, base, (row_peer(d), c), val_sem.at[step, d - 1])

        if step == 0:
            fill_spread(r, map_ref[...])
            fill_pick(r, map_ref[...])
            wait_bytes(map_in.at[pl.ds(0, rows - 1)], recv_sem.at[0])

            def fill_rest(d, _):
                fill_spread(row_peer(d), map_in[row_peer(d)])
                return 0

            lax.fori_loop(1, rows, fill_rest, 0)

        rhs = dot_nt(val_in[step, r], spread[r])
        for d in reversed(far_first):
            q = row_peer(rows - d)
            wait_bytes(val_in.at[step, q], val_sem.at[step, d - 1])
            rhs += dot_nt(val_in[step, q], spread[q])
        rhs = joined(rhs, scen).astype(BF16)
        for b in range(cols):
            rhs_send[step, b] = rhs[:, b * share : (b + 1) * share]

        def send_rhs(t, _):
            peer_r = lax.rem(r + t // cols, rows)
            peer_c = lax.rem(c + lax.rem(t, cols), cols)
            send(
                rhs_send.at[step, peer_c],
                rhs_in.at[step, r * cols + c],
                base + 1,
                (peer_r, peer_c),
            )
            return 0

        lax.fori_loop(1, rows * cols, send_rhs, 0)
        rhs_in[step, r * cols + c] = rhs_send[step, c]

        if step == 0:

            def fill_rest_pick(d, _):
                fill_pick(row_peer(d), map_in[row_peer(d)])
                return 0

            lax.fori_loop(1, rows, fill_rest_pick, 0)
            loads[-1].wait()

        wait_bytes(rhs_in.at[step, pl.ds(0, others)], recv_sem.at[base + 1])
        wide = jnp.concatenate(
            [
                rhs_in[step, q * cols : (q + 1) * cols].reshape(cols * scen, share)
                for q in range(rows)
            ],
            axis=1,
        )
        for h in range(PIECES):
            part = dot_nt(wide, schur[h * piece : (h + 1) * piece, :]).astype(BF16)
            part_send[step, h] = part.reshape(cols, scen, piece)
            for d in range(1, cols):
                peer = lax.rem(c + d, cols)
                send(
                    part_send.at[step, h, peer],
                    part_in.at[step, h, c],
                    base + 2 + h,
                    (r, peer),
                )
            part_in[step, h, c] = part_send[step, h, c]

        def summed(h):
            wait_bytes(part_in.at[step, h, pl.ds(0, cols - 1)], recv_sem.at[base + 2 + h])
            iface = part_in[step, h, 0].astype(F32)
            for b in range(1, cols):
                iface += part_in[step, h, b].astype(F32)
            if step == STEPS - 1:
                iface_out[:, h * piece : (h + 1) * piece] = iface
            return halves(iface)

        order = far_first + [0]
        totals = {}
        for h in range(PIECES):
            iface = summed(h)
            for d in order:
                q = row_peer(d)
                term = dot_nn(iface, pick[q, h * piece : (h + 1) * piece, :])
                totals[d] = term if h == 0 else totals[d] + term
                if h == PIECES - 1:
                    if d == 0:
                        pick_in[step, r] = totals[d].astype(BF16)
                    else:
                        pick_send[step, q] = totals[d].astype(BF16)
                        send(
                            pick_send.at[step, q],
                            pick_in.at[step, r],
                            base + 2 + PIECES,
                            (q, c),
                        )
        wait_bytes(pick_in.at[step, pl.ds(0, rows - 1)], recv_sem.at[base + 2 + PIECES])
        picked = joined(pick_in[step, 0], scen)
        for q in range(1, rows):
            picked += joined(pick_in[step, q], scen)

        drives = []
        for k in range(sub):
            first = (k % half) * LANES + (k // half) * ports
            drives.append((tie_ref[k : k + 1, :] * picked[:, first : first + ports]).astype(BF16))
        for k in range(sub):
            volt, curr = volt_now[k], curr_now[k]
            volt_next = open_volt[k] + dot_nn(drives[k], linv[k, :ports, :])
            closed = breaker_ref[k].astype(F32)
            curr_out[k] = closed * (curr + gain_ref[k : k + 1, :] * (volt_next + volt))
            volt_out[k] = volt_next

    wait_bytes(map_in.at[pl.ds(0, rows - 1)], send_sem.at[0])
    for step in range(STEPS):
        base = 1 + (3 + PIECES) * step
        wait_bytes(val_in.at[step, pl.ds(0, rows - 1)], send_sem.at[base])
        wait_bytes(rhs_in.at[step, pl.ds(0, others)], send_sem.at[base + 1])
        for h in range(PIECES):
            wait_bytes(part_in.at[step, h, pl.ds(0, cols - 1)], send_sem.at[base + 2 + h])
        wait_bytes(pick_in.at[step, pl.ds(0, rows - 1)], send_sem.at[base + 2 + PIECES])


def fused(
    volt_init,
    curr_init,
    local_inverse,
    schur_inverse,
    ind_gain,
    tie,
    port_map,
    breaker,
    fault_time,
    fault_node,
):
    rows, cols = lax.axis_size("row"), lax.axis_size("col")
    sub, scen, nodes = volt_init.shape
    ports = tie.shape[1]
    own_i, own_j = schur_inverse.shape
    share = own_j // rows
    flat = sub * ports
    vmem = pl.BlockSpec(memory_space=pltpu.VMEM)
    hbm = pl.BlockSpec(memory_space=pltpu.HBM)
    return pl.pallas_call(
        functools.partial(kernel, rows, cols),
        out_shape=(
            jax.ShapeDtypeStruct(volt_init.shape, F32),
            jax.ShapeDtypeStruct(volt_init.shape, F32),
            jax.ShapeDtypeStruct((scen, own_i), F32),
        ),
        in_specs=[hbm] * 10,
        out_specs=(vmem, vmem, vmem),
        scratch_shapes=[
            pltpu.VMEM(volt_init.shape, F32),
            pltpu.VMEM(volt_init.shape, F32),
            pltpu.VMEM(local_inverse.shape, BF16),
            pltpu.VMEM(schur_inverse.shape, BF16),
            pltpu.VMEM(ind_gain.shape, F32),
            pltpu.VMEM(tie.shape, F32),
            pltpu.VMEM(port_map.shape, jnp.int32),
            pltpu.VMEM(breaker.shape, jnp.int32),
            pltpu.SMEM(fault_time.shape, jnp.int32),
            pltpu.SMEM(fault_node.shape, jnp.int32),
            pltpu.VMEM(volt_init.shape, F32),
            pltpu.VMEM((rows, sub, ports), jnp.int32),
            pltpu.VMEM((rows, cols * share, flat), BF16),
            pltpu.VMEM((rows, own_i, flat), BF16),
            pltpu.VMEM((STEPS, rows, 2 * scen, flat), BF16),
            pltpu.VMEM((STEPS, cols, scen, share), BF16),
            pltpu.VMEM((STEPS, rows * cols, scen, share), BF16),
            pltpu.VMEM((STEPS, PIECES, cols, scen, own_i // PIECES), BF16),
            pltpu.VMEM((STEPS, PIECES, cols, scen, own_i // PIECES), BF16),
            pltpu.VMEM((STEPS, rows, 2 * scen, flat), BF16),
            pltpu.VMEM((STEPS, rows, 2 * scen, flat), BF16),
            pltpu.SemaphoreType.DMA((10,)),
            pltpu.SemaphoreType.DMA((1 + (3 + PIECES) * STEPS,)),
            pltpu.SemaphoreType.DMA((1 + (3 + PIECES) * STEPS,)),
            pltpu.SemaphoreType.DMA((STEPS, rows - 1)),
        ],
        compiler_params=pltpu.CompilerParams(
            collective_id=0, has_side_effects=True, vmem_limit_bytes=60 * 1024 * 1024
        ),
    )(
        volt_init,
        curr_init,
        local_inverse,
        schur_inverse,
        ind_gain,
        tie,
        port_map,
        breaker,
        fault_time,
        fault_node,
    )


def plain(
    volt_init,
    curr_init,
    local_inverse,
    schur_inverse,
    ind_gain,
    tie,
    port_map,
    breaker,
    fault_time,
    fault_node,
):
    sub_count, scen_count, node_count = volt_init.shape
    port_count = tie.shape[1]
    iface_width = lax.axis_size("row") * schur_inverse.shape[0]
    volt = volt_init
    curr = curr_init
    closed = breaker.astype(F32)
    first_sub = lax.axis_index("row") * sub_count
    node_ids = (first_sub + jnp.arange(sub_count, dtype=jnp.int32))[
        :, None
    ] * node_count + jnp.arange(node_count, dtype=jnp.int32)[None, :]
    hits = node_ids[:, None, :] == fault_node[None, :, None]
    flat_map = port_map.reshape(-1)
    port_inverse = local_inverse[:, :port_count, :]
    iface_block = jnp.zeros((scen_count, schur_inverse.shape[0]), F32)
    for step in range(STEPS):
        hist = closed * (curr + ind_gain[:, None, :] * volt)
        active = (step >= fault_time)[None, :, None]
        fault_on = jnp.where(hits & active, 1.0, 0.0).astype(F32)
        inject = (-hist - 2.0 * fault_on * volt).astype(BF16)
        open_volt = jnp.einsum("ksn,knm->ksm", inject, local_inverse, preferred_element_type=F32)
        values = tie[:, None, :] * open_volt[:, :, :port_count]
        flat_values = jnp.transpose(values, (0, 2, 1)).reshape(sub_count * port_count, scen_count)
        partial_rhs = jax.ops.segment_sum(flat_values, flat_map, iface_width).T
        owned = lax.psum_scatter(partial_rhs, "row", scatter_dimension=1, tiled=True)
        rhs_half = lax.all_gather(owned.astype(BF16), "row", axis=1, tiled=True)
        iface_block = dot_nt(rhs_half, lax.all_gather(schur_inverse, "col", axis=1, tiled=True))
        iface_full = lax.all_gather(iface_block, "row", axis=1, tiled=True)
        picked = jnp.take(iface_full, flat_map, axis=1).reshape(scen_count, sub_count, port_count)
        drive = (tie[:, None, :] * jnp.transpose(picked, (1, 0, 2))).astype(BF16)
        volt_next = open_volt + jnp.einsum(
            "ksp,kpn->ksn", drive, port_inverse, preferred_element_type=F32
        )
        curr = closed * (curr + ind_gain[:, None, :] * (volt_next + volt))
        volt = volt_next
    return (volt, curr, iface_block)


def local(*args):
    volt_init, schur_inverse, tie = args[0], args[3], args[5]
    sub, scen, _ = volt_init.shape
    own_i, own_j = schur_inverse.shape
    aligned = (
        own_j % (lax.axis_size("row") * LANES) == 0
        and own_i % (PIECES * LANES) == 0
        and scen % 16 == 0
        and sub % 2 == 0
        and 2 * tie.shape[1] == LANES
    )
    return fused(*args) if aligned else plain(*args)


def solution(mesh):
    placed = (
        P("row", "col", None),
        P("row", "col", None),
        P("row", None, None),
        P("row", "col"),
        P("row", None),
        P("row", None),
        P("row", None),
        P("row", "col", None),
        P("col"),
        P("col"),
    )
    return jax.shard_map(
        local,
        mesh=mesh,
        in_specs=placed,
        out_specs=(P("row", "col", None), P("row", "col", None), P("col", "row")),
        check_vma=False,
    )
```

```python
import functools

import jax
import jax.numpy as jnp
from jax import lax
from jax.experimental import pallas as pl
from jax.experimental.pallas import tpu as pltpu
from jax.sharding import PartitionSpec as P

STEPS = 2
PIECES = 2
LANES = 128
MESH = pl.DeviceIdType.MESH
F32 = jnp.float32
BF16 = jnp.bfloat16


def halves(x):
    high = x.astype(BF16)
    low = (x - high.astype(F32)).astype(BF16)
    return jnp.concatenate([high, low], axis=0)


def joined(x, count):
    return x[:count].astype(F32) + x[count:].astype(F32)


def dot_nt(a, b):
    return lax.dot_general(a, b, (((1,), (1,)), ((), ())), preferred_element_type=F32)


def dot_nn(a, b):
    return lax.dot_general(a, b, (((1,), (0,)), ((), ())), preferred_element_type=F32)


def kernel(
    rows,
    cols,
    volt_hbm,
    curr_hbm,
    linv_hbm,
    schur_hbm,
    gain_hbm,
    tie_hbm,
    map_hbm,
    breaker_hbm,
    time_hbm,
    node_hbm,
    volt_out,
    curr_out,
    iface_out,
    volt_ref,
    curr_ref,
    linv,
    schur,
    gain_ref,
    tie_ref,
    map_ref,
    breaker_ref,
    time_ref,
    node_ref,
    open_volt,
    map_in,
    spread,
    pick,
    val_in,
    rhs_send,
    rhs_in,
    part_send,
    part_in,
    pick_send,
    pick_in,
    load_sem,
    send_sem,
    recv_sem,
    val_sem,
):
    sub, scen, nodes = volt_ref.shape
    ports = tie_ref.shape[1]
    half = sub // 2
    own_i, own_j = schur.shape
    share = own_j // rows
    piece = own_i // PIECES
    r = lax.axis_index("row")
    c = lax.axis_index("col")

    loads = [
        pltpu.make_async_copy(src, dst, load_sem.at[n])
        for n, (src, dst) in enumerate(
            (
                (time_hbm, time_ref),
                (node_hbm, node_ref),
                (gain_hbm, gain_ref),
                (tie_hbm, tie_ref),
                (map_hbm, map_ref),
                (volt_hbm, volt_ref),
                (curr_hbm, curr_ref),
                (breaker_hbm, breaker_ref),
                (linv_hbm, linv),
                (schur_hbm, schur),
            )
        )
    ]
    for load in loads:
        load.start()

    barrier = pltpu.get_barrier_semaphore()

    friends = [(lax.rem(r + d, rows), c) for d in range(1, rows)]
    friends += [(r, lax.rem(c + d, cols)) for d in range(1, cols)]
    for there in friends:
        pl.semaphore_signal(barrier, inc=1, device_id=there, device_id_type=MESH)
    for load in loads[:-1]:
        load.wait()

    def wait_bytes(ref, sem):
        pltpu.make_async_copy(ref, ref, sem).wait()

    def send(src, dst, phase, there, recv=None):
        pltpu.make_async_remote_copy(
            src_ref=src,
            dst_ref=dst,
            send_sem=send_sem.at[phase],
            recv_sem=recv_sem.at[phase] if recv is None else recv,
            device_id=there,
            device_id_type=MESH,
        ).start()

    def row_peer(d):
        return lax.rem(r + d, rows)

    far_first = sorted(range(1, rows), key=lambda d: abs(d - rows // 2))

    scen_ids = lax.broadcasted_iota(jnp.int32, (scen, 1), 0)
    f_node = jnp.zeros((scen, 1), jnp.int32)
    f_time = jnp.zeros((scen, 1), jnp.int32)
    for s in range(scen):
        f_node = jnp.where(scen_ids == s, node_ref[s], f_node)
        f_time = jnp.where(scen_ids == s, time_ref[s], f_time)
    node_ids = lax.broadcasted_iota(jnp.int32, (scen, nodes), 1)

    def injection(step, k, volt, curr):
        closed = breaker_ref[k].astype(F32)
        hist = closed * (curr + gain_ref[k : k + 1, :] * volt)
        here = f_node - (r * sub + k) * nodes
        on = jnp.logical_and(node_ids == here, f_time <= step)
        fault_on = jnp.where(on, 1.0, 0.0).astype(F32)
        return (-hist - 2.0 * fault_on * volt).astype(BF16)

    ids = lax.broadcasted_iota(jnp.int32, (LANES, LANES), 0).astype(F32).astype(BF16)
    one = jnp.ones((LANES, LANES), BF16)
    zero = jnp.zeros((LANES, LANES), BF16)

    def hits(m):
        near = jnp.clip(m, -1, LANES).astype(F32).astype(BF16)
        return jnp.where(ids == near, one, zero)

    def packed_map(m, g):
        return jnp.concatenate([m[g : g + 1], m[g + half : g + half + 1]], axis=1)

    def fill_spread(q, maps):
        for g in range(half):
            m = packed_map(maps, g)
            for b in range(cols):
                for e in range(share // LANES):
                    first = b * share + e * LANES
                    spread[q, first : first + LANES, g * LANES : (g + 1) * LANES] = hits(
                        m - (b * own_j + r * share + e * LANES)
                    )

    def fill_pick(q, maps):
        for g in range(half):
            m = packed_map(maps, g) - r * own_i
            for e in range(own_i // LANES):
                pick[q, e * LANES : (e + 1) * LANES, g * LANES : (g + 1) * LANES] = hits(
                    m - e * LANES
                )

    for step in range(STEPS):
        base = 1 + (4 + PIECES) * step
        volt_now, curr_now = (volt_ref, curr_ref) if step == 0 else (volt_out, curr_out)
        injects = [injection(step, k, volt_now[k], curr_now[k]) for k in range(sub)]
        for k in range(sub):
            open_volt[k] = dot_nn(injects[k], linv[k])

        def port_values(k):
            return tie_ref[k : k + 1, :] * open_volt[k, :, :ports]

        vals = jnp.concatenate(
            [
                jnp.concatenate([port_values(g), port_values(g + half)], axis=1)
                for g in range(half)
            ],
            axis=1,
        )
        val_in[step, r] = halves(vals)
        if step == 0:
            pl.semaphore_wait(barrier, len(friends))
            for d in far_first:
                send(map_ref, map_in.at[r], 0, (row_peer(d), c))
        for d in far_first:
            mine = val_in.at[step, r]
            send(mine, mine, base, (row_peer(d), c), val_sem.at[step, d - 1])

        if step == 0:
            fill_spread(r, map_ref[...])
            fill_pick(r, map_ref[...])
            wait_bytes(map_in.at[pl.ds(0, rows - 1)], recv_sem.at[0])

            def fill_rest(d, _):
                fill_spread(row_peer(d), map_in[row_peer(d)])
                return 0

            lax.fori_loop(1, rows, fill_rest, 0)

        rhs = dot_nt(val_in[step, r], spread[r])
        for d in reversed(far_first):
            q = row_peer(rows - d)
            wait_bytes(val_in.at[step, q], val_sem.at[step, d - 1])
            rhs += dot_nt(val_in[step, q], spread[q])
        rhs = joined(rhs, scen).astype(BF16)
        for b in range(cols):
            rhs_send[step, b] = rhs[:, b * share : (b + 1) * share]

        for d in range(1, cols):
            peer = lax.rem(c + d, cols)
            send(rhs_send.at[step, peer], rhs_in.at[step, r, c], base + 1, (r, peer))
        rhs_in[step, r, c] = rhs_send[step, c]

        if step == 0:

            def fill_rest_pick(d, _):
                fill_pick(row_peer(d), map_in[row_peer(d)])
                return 0

            lax.fori_loop(1, rows, fill_rest_pick, 0)
            loads[-1].wait()

        wait_bytes(rhs_in.at[step, r, pl.ds(0, cols - 1)], recv_sem.at[base + 1])
        for d in far_first:
            mine = rhs_in.at[step, r]
            send(mine, mine, base + 2, (row_peer(d), c))
        wait_bytes(rhs_in.at[step, pl.ds(0, rows - 1)], recv_sem.at[base + 2])
        wide = jnp.concatenate(
            [rhs_in[step, q].reshape(cols * scen, share) for q in range(rows)], axis=1
        )
        for h in range(PIECES):
            part = dot_nt(wide, schur[h * piece : (h + 1) * piece, :]).astype(BF16)
            part_send[step, h] = part.reshape(cols, scen, piece)
            for d in range(1, cols):
                peer = lax.rem(c + d, cols)
                send(
                    part_send.at[step, h, peer],
                    part_in.at[step, h, c],
                    base + 3 + h,
                    (r, peer),
                )
            part_in[step, h, c] = part_send[step, h, c]

        def summed(h):
            wait_bytes(part_in.at[step, h, pl.ds(0, cols - 1)], recv_sem.at[base + 3 + h])
            iface = part_in[step, h, 0].astype(F32)
            for b in range(1, cols):
                iface += part_in[step, h, b].astype(F32)
            if step == STEPS - 1:
                iface_out[:, h * piece : (h + 1) * piece] = iface
            return halves(iface)

        order = far_first + [0]
        totals = {}
        for h in range(PIECES):
            iface = summed(h)
            for d in order:
                q = row_peer(d)
                term = dot_nn(iface, pick[q, h * piece : (h + 1) * piece, :])
                totals[d] = term if h == 0 else totals[d] + term
                if h == PIECES - 1:
                    if d == 0:
                        pick_in[step, r] = totals[d].astype(BF16)
                    else:
                        pick_send[step, q] = totals[d].astype(BF16)
                        send(
                            pick_send.at[step, q],
                            pick_in.at[step, r],
                            base + 3 + PIECES,
                            (q, c),
                        )
        wait_bytes(pick_in.at[step, pl.ds(0, rows - 1)], recv_sem.at[base + 3 + PIECES])
        picked = joined(pick_in[step, 0], scen)
        for q in range(1, rows):
            picked += joined(pick_in[step, q], scen)

        drives = []
        for k in range(sub):
            first = (k % half) * LANES + (k // half) * ports
            drives.append((tie_ref[k : k + 1, :] * picked[:, first : first + ports]).astype(BF16))
        for k in range(sub):
            volt, curr = volt_now[k], curr_now[k]
            volt_next = open_volt[k] + dot_nn(drives[k], linv[k, :ports, :])
            closed = breaker_ref[k].astype(F32)
            curr_out[k] = closed * (curr + gain_ref[k : k + 1, :] * (volt_next + volt))
            volt_out[k] = volt_next

    wait_bytes(map_in.at[pl.ds(0, rows - 1)], send_sem.at[0])
    for step in range(STEPS):
        base = 1 + (4 + PIECES) * step
        wait_bytes(val_in.at[step, pl.ds(0, rows - 1)], send_sem.at[base])
        wait_bytes(rhs_in.at[step, 0, pl.ds(0, cols - 1)], send_sem.at[base + 1])
        wait_bytes(rhs_in.at[step, pl.ds(0, rows - 1)], send_sem.at[base + 2])
        for h in range(PIECES):
            wait_bytes(part_in.at[step, h, pl.ds(0, cols - 1)], send_sem.at[base + 3 + h])
        wait_bytes(pick_in.at[step, pl.ds(0, rows - 1)], send_sem.at[base + 3 + PIECES])


def fused(
    volt_init,
    curr_init,
    local_inverse,
    schur_inverse,
    ind_gain,
    tie,
    port_map,
    breaker,
    fault_time,
    fault_node,
):
    rows, cols = lax.axis_size("row"), lax.axis_size("col")
    sub, scen, nodes = volt_init.shape
    ports = tie.shape[1]
    own_i, own_j = schur_inverse.shape
    share = own_j // rows
    flat = sub * ports
    vmem = pl.BlockSpec(memory_space=pltpu.VMEM)
    hbm = pl.BlockSpec(memory_space=pltpu.HBM)
    return pl.pallas_call(
        functools.partial(kernel, rows, cols),
        out_shape=(
            jax.ShapeDtypeStruct(volt_init.shape, F32),
            jax.ShapeDtypeStruct(volt_init.shape, F32),
            jax.ShapeDtypeStruct((scen, own_i), F32),
        ),
        in_specs=[hbm] * 10,
        out_specs=(vmem, vmem, vmem),
        scratch_shapes=[
            pltpu.VMEM(volt_init.shape, F32),
            pltpu.VMEM(volt_init.shape, F32),
            pltpu.VMEM(local_inverse.shape, BF16),
            pltpu.VMEM(schur_inverse.shape, BF16),
            pltpu.VMEM(ind_gain.shape, F32),
            pltpu.VMEM(tie.shape, F32),
            pltpu.VMEM(port_map.shape, jnp.int32),
            pltpu.VMEM(breaker.shape, jnp.int32),
            pltpu.SMEM(fault_time.shape, jnp.int32),
            pltpu.SMEM(fault_node.shape, jnp.int32),
            pltpu.VMEM(volt_init.shape, F32),
            pltpu.VMEM((rows, sub, ports), jnp.int32),
            pltpu.VMEM((rows, cols * share, flat), BF16),
            pltpu.VMEM((rows, own_i, flat), BF16),
            pltpu.VMEM((STEPS, rows, 2 * scen, flat), BF16),
            pltpu.VMEM((STEPS, cols, scen, share), BF16),
            pltpu.VMEM((STEPS, rows, cols, scen, share), BF16),
            pltpu.VMEM((STEPS, PIECES, cols, scen, own_i // PIECES), BF16),
            pltpu.VMEM((STEPS, PIECES, cols, scen, own_i // PIECES), BF16),
            pltpu.VMEM((STEPS, rows, 2 * scen, flat), BF16),
            pltpu.VMEM((STEPS, rows, 2 * scen, flat), BF16),
            pltpu.SemaphoreType.DMA((10,)),
            pltpu.SemaphoreType.DMA((1 + (4 + PIECES) * STEPS,)),
            pltpu.SemaphoreType.DMA((1 + (4 + PIECES) * STEPS,)),
            pltpu.SemaphoreType.DMA((STEPS, rows - 1)),
        ],
        compiler_params=pltpu.CompilerParams(
            collective_id=0, has_side_effects=True, vmem_limit_bytes=60 * 1024 * 1024
        ),
    )(
        volt_init,
        curr_init,
        local_inverse,
        schur_inverse,
        ind_gain,
        tie,
        port_map,
        breaker,
        fault_time,
        fault_node,
    )


def plain(
    volt_init,
    curr_init,
    local_inverse,
    schur_inverse,
    ind_gain,
    tie,
    port_map,
    breaker,
    fault_time,
    fault_node,
):
    sub_count, scen_count, node_count = volt_init.shape
    port_count = tie.shape[1]
    iface_width = lax.axis_size("row") * schur_inverse.shape[0]
    volt = volt_init
    curr = curr_init
    closed = breaker.astype(F32)
    first_sub = lax.axis_index("row") * sub_count
    node_ids = (first_sub + jnp.arange(sub_count, dtype=jnp.int32))[
        :, None
    ] * node_count + jnp.arange(node_count, dtype=jnp.int32)[None, :]
    hits = node_ids[:, None, :] == fault_node[None, :, None]
    flat_map = port_map.reshape(-1)
    port_inverse = local_inverse[:, :port_count, :]
    iface_block = jnp.zeros((scen_count, schur_inverse.shape[0]), F32)
    for step in range(STEPS):
        hist = closed * (curr + ind_gain[:, None, :] * volt)
        active = (step >= fault_time)[None, :, None]
        fault_on = jnp.where(hits & active, 1.0, 0.0).astype(F32)
        inject = (-hist - 2.0 * fault_on * volt).astype(BF16)
        open_volt = jnp.einsum("ksn,knm->ksm", inject, local_inverse, preferred_element_type=F32)
        values = tie[:, None, :] * open_volt[:, :, :port_count]
        flat_values = jnp.transpose(values, (0, 2, 1)).reshape(sub_count * port_count, scen_count)
        partial_rhs = jax.ops.segment_sum(flat_values, flat_map, iface_width).T
        owned = lax.psum_scatter(partial_rhs, "row", scatter_dimension=1, tiled=True)
        rhs_half = lax.all_gather(owned.astype(BF16), "row", axis=1, tiled=True)
        iface_block = dot_nt(rhs_half, lax.all_gather(schur_inverse, "col", axis=1, tiled=True))
        iface_full = lax.all_gather(iface_block, "row", axis=1, tiled=True)
        picked = jnp.take(iface_full, flat_map, axis=1).reshape(scen_count, sub_count, port_count)
        drive = (tie[:, None, :] * jnp.transpose(picked, (1, 0, 2))).astype(BF16)
        volt_next = open_volt + jnp.einsum(
            "ksp,kpn->ksn", drive, port_inverse, preferred_element_type=F32
        )
        curr = closed * (curr + ind_gain[:, None, :] * (volt_next + volt))
        volt = volt_next
    return (volt, curr, iface_block)


def local(*args):
    volt_init, schur_inverse, tie = args[0], args[3], args[5]
    sub, scen, _ = volt_init.shape
    own_i, own_j = schur_inverse.shape
    aligned = (
        own_j % (lax.axis_size("row") * LANES) == 0
        and own_i % (PIECES * LANES) == 0
        and scen % 16 == 0
        and sub % 2 == 0
        and 2 * tie.shape[1] == LANES
    )
    return fused(*args) if aligned else plain(*args)


def solution(mesh):
    placed = (
        P("row", "col", None),
        P("row", "col", None),
        P("row", None, None),
        P("row", "col"),
        P("row", None),
        P("row", None),
        P("row", None),
        P("row", "col", None),
        P("col"),
        P("col"),
    )
    return jax.shard_map(
        local,
        mesh=mesh,
        in_specs=placed,
        out_specs=(P("row", "col", None), P("row", "col", None), P("col", "row")),
        check_vma=False,
    )
```

```python
import functools

import jax
import jax.numpy as jnp
from jax import lax
from jax.experimental import pallas as pl
from jax.experimental.pallas import tpu as pltpu
from jax.sharding import PartitionSpec as P

STEPS = 2
PIECES = 2
LANES = 128
MESH = pl.DeviceIdType.MESH
F32 = jnp.float32
BF16 = jnp.bfloat16


def halves(x):
    high = x.astype(BF16)
    low = (x - high.astype(F32)).astype(BF16)
    return jnp.concatenate([high, low], axis=0)


def joined(x, count):
    return x[:count].astype(F32) + x[count:].astype(F32)


def dot_nt(a, b):
    return lax.dot_general(a, b, (((1,), (1,)), ((), ())), preferred_element_type=F32)


def dot_nn(a, b):
    return lax.dot_general(a, b, (((1,), (0,)), ((), ())), preferred_element_type=F32)


def kernel(
    rows,
    cols,
    volt_hbm,
    curr_hbm,
    linv_hbm,
    schur_hbm,
    gain_hbm,
    tie_hbm,
    map_hbm,
    breaker_hbm,
    time_hbm,
    node_hbm,
    volt_out,
    curr_out,
    open_out,
    picked_out,
    iface_out,
    volt_ref,
    curr_ref,
    linv,
    schur,
    gain_ref,
    tie_ref,
    map_ref,
    breaker_ref,
    time_ref,
    node_ref,
    open_volt,
    map_in,
    spread,
    pick,
    val_in,
    rhs_send,
    rhs_in,
    part_send,
    part_in,
    pick_send,
    pick_in,
    picked_ref,
    iface_ref,
    load_sem,
    store_sem,
    send_sem,
    recv_sem,
    val_sem,
):
    sub, scen, nodes = volt_ref.shape
    ports = tie_ref.shape[1]
    half = sub // 2
    own_i, own_j = schur.shape
    share = own_j // rows
    piece = own_i // PIECES
    r = lax.axis_index("row")
    c = lax.axis_index("col")
    others = rows * cols - 1

    loads = [
        pltpu.make_async_copy(src, dst, load_sem.at[n])
        for n, (src, dst) in enumerate(
            (
                (time_hbm, time_ref),
                (node_hbm, node_ref),
                (gain_hbm, gain_ref),
                (tie_hbm, tie_ref),
                (map_hbm, map_ref),
                (volt_hbm, volt_ref),
                (curr_hbm, curr_ref),
                (breaker_hbm, breaker_ref),
                (linv_hbm, linv),
                (schur_hbm, schur),
            )
        )
    ]
    for load in loads:
        load.start()

    barrier = pltpu.get_barrier_semaphore()

    def greet(t, _):
        there = (lax.rem(r + t // cols, rows), lax.rem(c + lax.rem(t, cols), cols))
        pl.semaphore_signal(barrier, inc=1, device_id=there, device_id_type=MESH)
        return 0

    lax.fori_loop(1, rows * cols, greet, 0)
    for load in loads[:-1]:
        load.wait()

    def wait_bytes(ref, sem):
        pltpu.make_async_copy(ref, ref, sem).wait()

    def send(src, dst, phase, there, recv=None):
        pltpu.make_async_remote_copy(
            src_ref=src,
            dst_ref=dst,
            send_sem=send_sem.at[phase],
            recv_sem=recv_sem.at[phase] if recv is None else recv,
            device_id=there,
            device_id_type=MESH,
        ).start()

    def row_peer(d):
        return lax.rem(r + d, rows)

    far_first = sorted(range(1, rows), key=lambda d: abs(d - rows // 2))

    scen_ids = lax.broadcasted_iota(jnp.int32, (scen, 1), 0)
    f_node = jnp.zeros((scen, 1), jnp.int32)
    f_time = jnp.zeros((scen, 1), jnp.int32)
    for s in range(scen):
        f_node = jnp.where(scen_ids == s, node_ref[s], f_node)
        f_time = jnp.where(scen_ids == s, time_ref[s], f_time)
    node_ids = lax.broadcasted_iota(jnp.int32, (scen, nodes), 1)

    def injection(step, k, volt, curr):
        closed = breaker_ref[k].astype(F32)
        hist = closed * (curr + gain_ref[k : k + 1, :] * volt)
        here = f_node - (r * sub + k) * nodes
        on = jnp.logical_and(node_ids == here, f_time <= step)
        fault_on = jnp.where(on, 1.0, 0.0).astype(F32)
        return (-hist - 2.0 * fault_on * volt).astype(BF16)

    ids = lax.broadcasted_iota(jnp.int32, (LANES, LANES), 0).astype(F32).astype(BF16)
    one = jnp.ones((LANES, LANES), BF16)
    zero = jnp.zeros((LANES, LANES), BF16)

    def hits(m):
        near = jnp.clip(m, -1, LANES).astype(F32).astype(BF16)
        return jnp.where(ids == near, one, zero)

    def packed_map(m, g):
        return jnp.concatenate([m[g : g + 1], m[g + half : g + half + 1]], axis=1)

    def fill_spread(q, maps):
        for g in range(half):
            m = packed_map(maps, g)
            for b in range(cols):
                for e in range(share // LANES):
                    first = b * share + e * LANES
                    spread[q, first : first + LANES, g * LANES : (g + 1) * LANES] = hits(
                        m - (b * own_j + r * share + e * LANES)
                    )

    def fill_pick(q, maps):
        for g in range(half):
            m = packed_map(maps, g) - r * own_i
            for e in range(own_i // LANES):
                pick[q, e * LANES : (e + 1) * LANES, g * LANES : (g + 1) * LANES] = hits(
                    m - e * LANES
                )

    stores = []

    def store(src, dst):
        copy = pltpu.make_async_copy(src, dst, store_sem.at[len(stores)])
        copy.start()
        stores.append(copy)

    for step in range(STEPS):
        base = 1 + (3 + PIECES) * step
        last = step == STEPS - 1
        injects = [injection(step, k, volt_ref[k], curr_ref[k]) for k in range(sub)]
        for k in range(sub):
            open_volt[k] = dot_nn(injects[k], linv[k])

        def port_values(k):
            return tie_ref[k : k + 1, :] * open_volt[k, :, :ports]

        vals = jnp.concatenate(
            [
                jnp.concatenate([port_values(g), port_values(g + half)], axis=1)
                for g in range(half)
            ],
            axis=1,
        )
        val_in[step, r] = halves(vals)
        if last:
            store(volt_ref, volt_out)
            store(curr_ref, curr_out)
            store(open_volt, open_out)
        if step == 0:
            pl.semaphore_wait(barrier, others)
            for d in far_first:
                send(map_ref, map_in.at[r], 0, (row_peer(d), c))
        for d in far_first:
            mine = val_in.at[step, r]
            send(mine, mine, base, (row_peer(d), c), val_sem.at[step, d - 1])

        if step == 0:
            fill_spread(r, map_ref[...])
            fill_pick(r, map_ref[...])
            wait_bytes(map_in.at[pl.ds(0, rows - 1)], recv_sem.at[0])

            def fill_rest(d, _):
                fill_spread(row_peer(d), map_in[row_peer(d)])
                return 0

            lax.fori_loop(1, rows, fill_rest, 0)

        rhs = dot_nt(val_in[step, r], spread[r])
        for d in reversed(far_first):
            q = row_peer(rows - d)
            wait_bytes(val_in.at[step, q], val_sem.at[step, d - 1])
            rhs += dot_nt(val_in[step, q], spread[q])
        rhs = joined(rhs, scen).astype(BF16)
        for b in range(cols):
            rhs_send[step, b] = rhs[:, b * share : (b + 1) * share]

        def send_rhs(t, _):
            peer_r = lax.rem(r + t // cols, rows)
            peer_c = lax.rem(c + lax.rem(t, cols), cols)
            send(
                rhs_send.at[step, peer_c],
                rhs_in.at[step, r * cols + c],
                base + 1,
                (peer_r, peer_c),
            )
            return 0

        lax.fori_loop(1, rows * cols, send_rhs, 0)
        rhs_in[step, r * cols + c] = rhs_send[step, c]

        if step == 0:

            def fill_rest_pick(d, _):
                fill_pick(row_peer(d), map_in[row_peer(d)])
                return 0

            lax.fori_loop(1, rows, fill_rest_pick, 0)
            loads[-1].wait()

        wait_bytes(rhs_in.at[step, pl.ds(0, others)], recv_sem.at[base + 1])
        wide = jnp.concatenate(
            [
                rhs_in[step, q * cols : (q + 1) * cols].reshape(cols * scen, share)
                for q in range(rows)
            ],
            axis=1,
        )
        for h in range(PIECES):
            part = dot_nt(wide, schur[h * piece : (h + 1) * piece, :]).astype(BF16)
            part_send[step, h] = part.reshape(cols, scen, piece)
            for d in range(1, cols):
                peer = lax.rem(c + d, cols)
                send(
                    part_send.at[step, h, peer],
                    part_in.at[step, h, c],
                    base + 2 + h,
                    (r, peer),
                )
            part_in[step, h, c] = part_send[step, h, c]

        def summed(h):
            wait_bytes(part_in.at[step, h, pl.ds(0, cols - 1)], recv_sem.at[base + 2 + h])
            iface = part_in[step, h, 0].astype(F32)
            for b in range(1, cols):
                iface += part_in[step, h, b].astype(F32)
            if last:
                iface_ref[:, h * piece : (h + 1) * piece] = iface
            return halves(iface)

        order = far_first + [0]
        totals = {}
        for h in range(PIECES):
            iface = summed(h)
            for d in order:
                q = row_peer(d)
                term = dot_nn(iface, pick[q, h * piece : (h + 1) * piece, :])
                totals[d] = term if h == 0 else totals[d] + term
                if h == PIECES - 1:
                    if d == 0:
                        pick_in[step, r] = totals[d].astype(BF16)
                    else:
                        pick_send[step, q] = totals[d].astype(BF16)
                        send(
                            pick_send.at[step, q],
                            pick_in.at[step, r],
                            base + 2 + PIECES,
                            (q, c),
                        )
        if last:
            store(iface_ref, iface_out)
        wait_bytes(pick_in.at[step, pl.ds(0, rows - 1)], recv_sem.at[base + 2 + PIECES])
        picked = joined(pick_in[step, 0], scen)
        for q in range(1, rows):
            picked += joined(pick_in[step, q], scen)

        if last:
            picked_ref[...] = picked
            store(picked_ref, picked_out)
            break
        drives = []
        for k in range(sub):
            first = (k % half) * LANES + (k // half) * ports
            drives.append((tie_ref[k : k + 1, :] * picked[:, first : first + ports]).astype(BF16))
        for k in range(sub):
            volt, curr = volt_ref[k], curr_ref[k]
            volt_next = open_volt[k] + dot_nn(drives[k], linv[k, :ports, :])
            closed = breaker_ref[k].astype(F32)
            curr_ref[k] = closed * (curr + gain_ref[k : k + 1, :] * (volt_next + volt))
            volt_ref[k] = volt_next

    for copy in stores:
        copy.wait()
    wait_bytes(map_in.at[pl.ds(0, rows - 1)], send_sem.at[0])
    for step in range(STEPS):
        base = 1 + (3 + PIECES) * step
        wait_bytes(val_in.at[step, pl.ds(0, rows - 1)], send_sem.at[base])
        wait_bytes(rhs_in.at[step, pl.ds(0, others)], send_sem.at[base + 1])
        for h in range(PIECES):
            wait_bytes(part_in.at[step, h, pl.ds(0, cols - 1)], send_sem.at[base + 2 + h])
        wait_bytes(pick_in.at[step, pl.ds(0, rows - 1)], send_sem.at[base + 2 + PIECES])


def update_kernel(
    volt_hbm,
    curr_hbm,
    open_hbm,
    linv_hbm,
    gain_hbm,
    tie_hbm,
    breaker_hbm,
    picked_hbm,
    iface_hbm,
    volt_out,
    curr_out,
    iface_out,
    volt_ref,
    curr_ref,
    open_ref,
    linv,
    gain_ref,
    tie_ref,
    breaker_ref,
    picked_ref,
    load_sem,
):
    sub = volt_ref.shape[0]
    ports = tie_ref.shape[1]
    half = sub // 2
    pairs = (
        (linv_hbm.at[:, pl.ds(0, ports), :], linv),
        (picked_hbm, picked_ref),
        (tie_hbm, tie_ref),
        (gain_hbm, gain_ref),
        (open_hbm, open_ref),
        (volt_hbm, volt_ref),
        (curr_hbm, curr_ref),
        (breaker_hbm, breaker_ref),
        (iface_hbm, iface_out),
    )
    loads = [
        pltpu.make_async_copy(src, dst, load_sem.at[n]) for n, (src, dst) in enumerate(pairs)
    ]
    for load in loads:
        load.start()
    for load in loads:
        load.wait()
    for k in range(sub):
        first = (k % half) * LANES + (k // half) * ports
        drive = (tie_ref[k : k + 1, :] * picked_ref[:, first : first + ports]).astype(BF16)
        volt_next = open_ref[k] + dot_nn(drive, linv[k])
        closed = breaker_ref[k].astype(F32)
        curr_out[k] = closed * (curr_ref[k] + gain_ref[k : k + 1, :] * (volt_next + volt_ref[k]))
        volt_out[k] = volt_next


def fused(
    volt_init,
    curr_init,
    local_inverse,
    schur_inverse,
    ind_gain,
    tie,
    port_map,
    breaker,
    fault_time,
    fault_node,
):
    rows, cols = lax.axis_size("row"), lax.axis_size("col")
    sub, scen, nodes = volt_init.shape
    ports = tie.shape[1]
    own_i, own_j = schur_inverse.shape
    share = own_j // rows
    flat = sub * ports
    vmem = pl.BlockSpec(memory_space=pltpu.VMEM)
    hbm = pl.BlockSpec(memory_space=pltpu.HBM)
    state = jax.ShapeDtypeStruct(volt_init.shape, F32)
    iface_shape = jax.ShapeDtypeStruct((scen, own_i), F32)
    volt, curr, open_volt, picked, iface = pl.pallas_call(
        functools.partial(kernel, rows, cols),
        out_shape=(
            state,
            state,
            state,
            jax.ShapeDtypeStruct((scen, flat), F32),
            iface_shape,
        ),
        in_specs=[hbm] * 10,
        out_specs=(hbm,) * 5,
        scratch_shapes=[
            pltpu.VMEM(volt_init.shape, F32),
            pltpu.VMEM(volt_init.shape, F32),
            pltpu.VMEM(local_inverse.shape, BF16),
            pltpu.VMEM(schur_inverse.shape, BF16),
            pltpu.VMEM(ind_gain.shape, F32),
            pltpu.VMEM(tie.shape, F32),
            pltpu.VMEM(port_map.shape, jnp.int32),
            pltpu.VMEM(breaker.shape, jnp.int32),
            pltpu.SMEM(fault_time.shape, jnp.int32),
            pltpu.SMEM(fault_node.shape, jnp.int32),
            pltpu.VMEM(volt_init.shape, F32),
            pltpu.VMEM((rows, sub, ports), jnp.int32),
            pltpu.VMEM((rows, cols * share, flat), BF16),
            pltpu.VMEM((rows, own_i, flat), BF16),
            pltpu.VMEM((STEPS, rows, 2 * scen, flat), BF16),
            pltpu.VMEM((STEPS, cols, scen, share), BF16),
            pltpu.VMEM((STEPS, rows * cols, scen, share), BF16),
            pltpu.VMEM((STEPS, PIECES, cols, scen, own_i // PIECES), BF16),
            pltpu.VMEM((STEPS, PIECES, cols, scen, own_i // PIECES), BF16),
            pltpu.VMEM((STEPS, rows, 2 * scen, flat), BF16),
            pltpu.VMEM((STEPS, rows, 2 * scen, flat), BF16),
            pltpu.VMEM((scen, flat), F32),
            pltpu.VMEM((scen, own_i), F32),
            pltpu.SemaphoreType.DMA((10,)),
            pltpu.SemaphoreType.DMA((5,)),
            pltpu.SemaphoreType.DMA((1 + (3 + PIECES) * STEPS,)),
            pltpu.SemaphoreType.DMA((1 + (3 + PIECES) * STEPS,)),
            pltpu.SemaphoreType.DMA((STEPS, rows - 1)),
        ],
        compiler_params=pltpu.CompilerParams(
            collective_id=0, has_side_effects=True, vmem_limit_bytes=60 * 1024 * 1024
        ),
    )(
        volt_init,
        curr_init,
        local_inverse,
        schur_inverse,
        ind_gain,
        tie,
        port_map,
        breaker,
        fault_time,
        fault_node,
    )
    return pl.pallas_call(
        update_kernel,
        out_shape=(state, state, iface_shape),
        in_specs=[hbm] * 9,
        out_specs=(vmem, vmem, vmem),
        scratch_shapes=[
            pltpu.VMEM(volt_init.shape, F32),
            pltpu.VMEM(volt_init.shape, F32),
            pltpu.VMEM(volt_init.shape, F32),
            pltpu.VMEM((sub, ports, nodes), BF16),
            pltpu.VMEM(ind_gain.shape, F32),
            pltpu.VMEM(tie.shape, F32),
            pltpu.VMEM(breaker.shape, jnp.int32),
            pltpu.VMEM((scen, flat), F32),
            pltpu.SemaphoreType.DMA((9,)),
        ],
        compiler_params=pltpu.CompilerParams(vmem_limit_bytes=60 * 1024 * 1024),
    )(volt, curr, open_volt, local_inverse, ind_gain, tie, breaker, picked, iface)


def plain(
    volt_init,
    curr_init,
    local_inverse,
    schur_inverse,
    ind_gain,
    tie,
    port_map,
    breaker,
    fault_time,
    fault_node,
):
    sub_count, scen_count, node_count = volt_init.shape
    port_count = tie.shape[1]
    iface_width = lax.axis_size("row") * schur_inverse.shape[0]
    volt = volt_init
    curr = curr_init
    closed = breaker.astype(F32)
    first_sub = lax.axis_index("row") * sub_count
    node_ids = (first_sub + jnp.arange(sub_count, dtype=jnp.int32))[
        :, None
    ] * node_count + jnp.arange(node_count, dtype=jnp.int32)[None, :]
    hits = node_ids[:, None, :] == fault_node[None, :, None]
    flat_map = port_map.reshape(-1)
    port_inverse = local_inverse[:, :port_count, :]
    iface_block = jnp.zeros((scen_count, schur_inverse.shape[0]), F32)
    for step in range(STEPS):
        hist = closed * (curr + ind_gain[:, None, :] * volt)
        active = (step >= fault_time)[None, :, None]
        fault_on = jnp.where(hits & active, 1.0, 0.0).astype(F32)
        inject = (-hist - 2.0 * fault_on * volt).astype(BF16)
        open_volt = jnp.einsum("ksn,knm->ksm", inject, local_inverse, preferred_element_type=F32)
        values = tie[:, None, :] * open_volt[:, :, :port_count]
        flat_values = jnp.transpose(values, (0, 2, 1)).reshape(sub_count * port_count, scen_count)
        partial_rhs = jax.ops.segment_sum(flat_values, flat_map, iface_width).T
        owned = lax.psum_scatter(partial_rhs, "row", scatter_dimension=1, tiled=True)
        rhs_half = lax.all_gather(owned.astype(BF16), "row", axis=1, tiled=True)
        iface_block = dot_nt(rhs_half, lax.all_gather(schur_inverse, "col", axis=1, tiled=True))
        iface_full = lax.all_gather(iface_block, "row", axis=1, tiled=True)
        picked = jnp.take(iface_full, flat_map, axis=1).reshape(scen_count, sub_count, port_count)
        drive = (tie[:, None, :] * jnp.transpose(picked, (1, 0, 2))).astype(BF16)
        volt_next = open_volt + jnp.einsum(
            "ksp,kpn->ksn", drive, port_inverse, preferred_element_type=F32
        )
        curr = closed * (curr + ind_gain[:, None, :] * (volt_next + volt))
        volt = volt_next
    return (volt, curr, iface_block)


def local(*args):
    volt_init, schur_inverse, tie = args[0], args[3], args[5]
    sub, scen, _ = volt_init.shape
    own_i, own_j = schur_inverse.shape
    aligned = (
        own_j % (lax.axis_size("row") * LANES) == 0
        and own_i % (PIECES * LANES) == 0
        and scen % 16 == 0
        and sub % 2 == 0
        and 2 * tie.shape[1] == LANES
    )
    return fused(*args) if aligned else plain(*args)


def solution(mesh):
    placed = (
        P("row", "col", None),
        P("row", "col", None),
        P("row", None, None),
        P("row", "col"),
        P("row", None),
        P("row", None),
        P("row", None),
        P("row", "col", None),
        P("col"),
        P("col"),
    )
    return jax.shard_map(
        local,
        mesh=mesh,
        in_specs=placed,
        out_specs=(P("row", "col", None), P("row", "col", None), P("col", "row")),
        check_vma=False,
    )
```

```python
import functools

import jax
import jax.numpy as jnp
from jax import lax
from jax.experimental import pallas as pl
from jax.experimental.pallas import tpu as pltpu
from jax.sharding import PartitionSpec as P

STEPS = 2
PIECES = 2
LANES = 128
MESH = pl.DeviceIdType.MESH
F32 = jnp.float32
BF16 = jnp.bfloat16


def halves(x):
    high = x.astype(BF16)
    low = (x - high.astype(F32)).astype(BF16)
    return jnp.concatenate([high, low], axis=0)


def joined(x, count):
    return x[:count].astype(F32) + x[count:].astype(F32)


def dot_nt(a, b):
    return lax.dot_general(a, b, (((1,), (1,)), ((), ())), preferred_element_type=F32)


def dot_nn(a, b):
    return lax.dot_general(a, b, (((1,), (0,)), ((), ())), preferred_element_type=F32)


def kernel(
    rows,
    cols,
    volt_hbm,
    curr_hbm,
    linv_hbm,
    schur_hbm,
    gain_hbm,
    tie_hbm,
    map_hbm,
    breaker_hbm,
    time_hbm,
    node_hbm,
    volt_out,
    curr_out,
    open_out,
    picked_out,
    iface_out,
    volt_ref,
    curr_ref,
    linv,
    schur,
    gain_ref,
    tie_ref,
    map_ref,
    breaker_ref,
    time_ref,
    node_ref,
    open_volt,
    map_in,
    spread,
    pick,
    val_in,
    rhs_send,
    rhs_in,
    part_send,
    part_in,
    pick_send,
    pick_in,
    picked_ref,
    iface_ref,
    load_sem,
    store_sem,
    send_sem,
    recv_sem,
    val_sem,
):
    sub, scen, nodes = volt_ref.shape
    ports = tie_ref.shape[1]
    half = sub // 2
    own_i, own_j = schur.shape
    share = own_j // rows
    piece = own_i // PIECES
    r = lax.axis_index("row")
    c = lax.axis_index("col")
    others = rows * cols - 1

    loads = [
        pltpu.make_async_copy(src, dst, load_sem.at[n])
        for n, (src, dst) in enumerate(
            (
                (time_hbm, time_ref),
                (node_hbm, node_ref),
                (gain_hbm, gain_ref),
                (tie_hbm, tie_ref),
                (map_hbm, map_ref),
                (volt_hbm, volt_ref),
                (curr_hbm, curr_ref),
                (breaker_hbm, breaker_ref),
                (linv_hbm, linv),
                (schur_hbm, schur),
            )
        )
    ]
    for load in loads:
        load.start()

    barrier = pltpu.get_barrier_semaphore()

    row_peers = [r] + [lax.rem(r + d, rows) for d in range(1, rows)]
    col_peers = [c] + [lax.rem(c + d, cols) for d in range(1, cols)]
    far_rows = sorted(range(1, rows), key=lambda d: abs(d - rows // 2))
    far_cols = sorted(range(1, cols), key=lambda d: abs(d - cols // 2))
    for e in far_cols + [0]:
        for d in far_rows + [0]:
            if d or e:
                pl.semaphore_signal(
                    barrier,
                    inc=1,
                    device_id=(row_peers[d], col_peers[e]),
                    device_id_type=MESH,
                )
    for load in loads[:-1]:
        load.wait()

    def wait_bytes(ref, sem):
        pltpu.make_async_copy(ref, ref, sem).wait()

    def send(src, dst, phase, there, recv=None):
        pltpu.make_async_remote_copy(
            src_ref=src,
            dst_ref=dst,
            send_sem=send_sem.at[phase],
            recv_sem=recv_sem.at[phase] if recv is None else recv,
            device_id=there,
            device_id_type=MESH,
        ).start()

    scen_ids = lax.broadcasted_iota(jnp.int32, (scen, 1), 0)
    f_node = jnp.zeros((scen, 1), jnp.int32)
    f_time = jnp.zeros((scen, 1), jnp.int32)
    for s in range(scen):
        f_node = jnp.where(scen_ids == s, node_ref[s], f_node)
        f_time = jnp.where(scen_ids == s, time_ref[s], f_time)
    node_ids = lax.broadcasted_iota(jnp.int32, (scen, nodes), 1)

    def injection(step, k, volt, curr):
        closed = breaker_ref[k].astype(F32)
        hist = closed * (curr + gain_ref[k : k + 1, :] * volt)
        here = f_node - (r * sub + k) * nodes
        on = jnp.logical_and(node_ids == here, f_time <= step)
        fault_on = jnp.where(on, 1.0, 0.0).astype(F32)
        return (-hist - 2.0 * fault_on * volt).astype(BF16)

    ids = lax.broadcasted_iota(jnp.int32, (LANES, LANES), 0).astype(F32).astype(BF16)
    one = jnp.ones((LANES, LANES), BF16)
    zero = jnp.zeros((LANES, LANES), BF16)

    def hits(m):
        near = jnp.clip(m, -1, LANES).astype(F32).astype(BF16)
        return jnp.where(ids == near, one, zero)

    def packed_map(m, g):
        return jnp.concatenate([m[g : g + 1], m[g + half : g + half + 1]], axis=1)

    def fill_spread(q, maps):
        for g in range(half):
            m = packed_map(maps, g)
            for b in range(cols):
                for e in range(share // LANES):
                    first = b * share + e * LANES
                    spread[q, first : first + LANES, g * LANES : (g + 1) * LANES] = hits(
                        m - (b * own_j + r * share + e * LANES)
                    )

    def fill_pick(q, maps):
        for g in range(half):
            m = packed_map(maps, g) - r * own_i
            for e in range(own_i // LANES):
                pick[q, e * LANES : (e + 1) * LANES, g * LANES : (g + 1) * LANES] = hits(
                    m - e * LANES
                )

    stores = []

    def store(src, dst):
        copy = pltpu.make_async_copy(src, dst, store_sem.at[len(stores)])
        copy.start()
        stores.append(copy)

    for step in range(STEPS):
        base = 1 + (3 + PIECES) * step
        last = step == STEPS - 1
        injects = [injection(step, k, volt_ref[k], curr_ref[k]) for k in range(sub)]
        for k in range(sub):
            open_volt[k] = dot_nn(injects[k], linv[k])

        def port_values(k):
            return tie_ref[k : k + 1, :] * open_volt[k, :, :ports]

        vals = jnp.concatenate(
            [
                jnp.concatenate([port_values(g), port_values(g + half)], axis=1)
                for g in range(half)
            ],
            axis=1,
        )
        val_in[step, r] = halves(vals)
        if last:
            store(volt_ref, volt_out)
            store(curr_ref, curr_out)
            store(open_volt, open_out)
        if step == 0:
            pl.semaphore_wait(barrier, others)
            for d in far_rows:
                send(map_ref, map_in.at[r], 0, (row_peers[d], c))
        for d in far_rows:
            mine = val_in.at[step, r]
            send(mine, mine, base, (row_peers[d], c), val_sem.at[step, d - 1])

        if step == 0:
            fill_spread(r, map_ref[...])
            wait_bytes(map_in.at[pl.ds(0, rows - 1)], recv_sem.at[0])

            def fill_rest(d, _):
                q = lax.rem(r + d, rows)
                fill_spread(q, map_in[q])
                return 0

            lax.fori_loop(1, rows, fill_rest, 0)

        rhs = dot_nt(val_in[step, r], spread[r])
        for d in reversed(far_rows):
            q = row_peers[rows - d]
            wait_bytes(val_in.at[step, q], val_sem.at[step, d - 1])
            rhs += dot_nt(val_in[step, q], spread[q])
        rhs = joined(rhs, scen).astype(BF16)
        for b in range(cols):
            rhs_send[step, b] = rhs[:, b * share : (b + 1) * share]

        for e in far_cols + [0]:
            for d in far_rows + [0]:
                if d or e:
                    send(
                        rhs_send.at[step, col_peers[e]],
                        rhs_in.at[step, r * cols + c],
                        base + 1,
                        (row_peers[d], col_peers[e]),
                    )
        rhs_in[step, r * cols + c] = rhs_send[step, c]

        if step == 0:

            fill_pick(r, map_ref[...])

            def fill_rest_pick(d, _):
                q = lax.rem(r + d, rows)
                fill_pick(q, map_in[q])
                return 0

            lax.fori_loop(1, rows, fill_rest_pick, 0)
            loads[-1].wait()

        wait_bytes(rhs_in.at[step, pl.ds(0, others)], recv_sem.at[base + 1])
        wide = jnp.concatenate(
            [
                rhs_in[step, q * cols : (q + 1) * cols].reshape(cols * scen, share)
                for q in range(rows)
            ],
            axis=1,
        )
        for h in range(PIECES):
            part = dot_nt(wide, schur[h * piece : (h + 1) * piece, :]).astype(BF16)
            part_send[step, h] = part.reshape(cols, scen, piece)
            for e in far_cols:
                peer = col_peers[e]
                send(
                    part_send.at[step, h, peer],
                    part_in.at[step, h, c],
                    base + 2 + h,
                    (r, peer),
                )
            part_in[step, h, c] = part_send[step, h, c]

        def summed(h):
            wait_bytes(part_in.at[step, h, pl.ds(0, cols - 1)], recv_sem.at[base + 2 + h])
            iface = part_in[step, h, 0].astype(F32)
            for b in range(1, cols):
                iface += part_in[step, h, b].astype(F32)
            if last:
                iface_ref[:, h * piece : (h + 1) * piece] = iface
            return halves(iface)

        order = far_rows + [0]
        totals = {}
        for h in range(PIECES):
            iface = summed(h)
            for d in order:
                q = row_peers[d]
                term = dot_nn(iface, pick[q, h * piece : (h + 1) * piece, :])
                totals[d] = term if h == 0 else totals[d] + term
                if h == PIECES - 1:
                    if d == 0:
                        pick_in[step, r] = totals[d].astype(BF16)
                    else:
                        pick_send[step, q] = totals[d].astype(BF16)
                        send(
                            pick_send.at[step, q],
                            pick_in.at[step, r],
                            base + 2 + PIECES,
                            (q, c),
                        )
        if last:
            store(iface_ref, iface_out)
        wait_bytes(pick_in.at[step, pl.ds(0, rows - 1)], recv_sem.at[base + 2 + PIECES])
        picked = joined(pick_in[step, 0], scen)
        for q in range(1, rows):
            picked += joined(pick_in[step, q], scen)

        if last:
            picked_ref[...] = picked
            store(picked_ref, picked_out)
            break
        drives = []
        for k in range(sub):
            first = (k % half) * LANES + (k // half) * ports
            drives.append((tie_ref[k : k + 1, :] * picked[:, first : first + ports]).astype(BF16))
        for k in range(sub):
            volt, curr = volt_ref[k], curr_ref[k]
            volt_next = open_volt[k] + dot_nn(drives[k], linv[k, :ports, :])
            closed = breaker_ref[k].astype(F32)
            curr_ref[k] = closed * (curr + gain_ref[k : k + 1, :] * (volt_next + volt))
            volt_ref[k] = volt_next

    for copy in stores:
        copy.wait()
    wait_bytes(map_in.at[pl.ds(0, rows - 1)], send_sem.at[0])
    for step in range(STEPS):
        base = 1 + (3 + PIECES) * step
        wait_bytes(val_in.at[step, pl.ds(0, rows - 1)], send_sem.at[base])
        wait_bytes(rhs_in.at[step, pl.ds(0, others)], send_sem.at[base + 1])
        for h in range(PIECES):
            wait_bytes(part_in.at[step, h, pl.ds(0, cols - 1)], send_sem.at[base + 2 + h])
        wait_bytes(pick_in.at[step, pl.ds(0, rows - 1)], send_sem.at[base + 2 + PIECES])


def update_kernel(
    volt_hbm,
    curr_hbm,
    open_hbm,
    linv_hbm,
    gain_hbm,
    tie_hbm,
    breaker_hbm,
    picked_hbm,
    iface_hbm,
    volt_out,
    curr_out,
    iface_out,
    volt_ref,
    curr_ref,
    open_ref,
    linv,
    gain_ref,
    tie_ref,
    breaker_ref,
    picked_ref,
    load_sem,
):
    sub = volt_ref.shape[0]
    ports = tie_ref.shape[1]
    half = sub // 2
    pairs = (
        (linv_hbm.at[:, pl.ds(0, ports), :], linv),
        (picked_hbm, picked_ref),
        (tie_hbm, tie_ref),
        (gain_hbm, gain_ref),
        (open_hbm, open_ref),
        (volt_hbm, volt_ref),
        (curr_hbm, curr_ref),
        (breaker_hbm, breaker_ref),
        (iface_hbm, iface_out),
    )
    loads = [
        pltpu.make_async_copy(src, dst, load_sem.at[n]) for n, (src, dst) in enumerate(pairs)
    ]
    for load in loads:
        load.start()
    for load in loads:
        load.wait()
    for k in range(sub):
        first = (k % half) * LANES + (k // half) * ports
        drive = (tie_ref[k : k + 1, :] * picked_ref[:, first : first + ports]).astype(BF16)
        volt_next = open_ref[k] + dot_nn(drive, linv[k])
        closed = breaker_ref[k].astype(F32)
        curr_out[k] = closed * (curr_ref[k] + gain_ref[k : k + 1, :] * (volt_next + volt_ref[k]))
        volt_out[k] = volt_next


def fused(
    volt_init,
    curr_init,
    local_inverse,
    schur_inverse,
    ind_gain,
    tie,
    port_map,
    breaker,
    fault_time,
    fault_node,
):
    rows, cols = lax.axis_size("row"), lax.axis_size("col")
    sub, scen, nodes = volt_init.shape
    ports = tie.shape[1]
    own_i, own_j = schur_inverse.shape
    share = own_j // rows
    flat = sub * ports
    vmem = pl.BlockSpec(memory_space=pltpu.VMEM)
    hbm = pl.BlockSpec(memory_space=pltpu.HBM)
    state = jax.ShapeDtypeStruct(volt_init.shape, F32)
    iface_shape = jax.ShapeDtypeStruct((scen, own_i), F32)
    volt, curr, open_volt, picked, iface = pl.pallas_call(
        functools.partial(kernel, rows, cols),
        out_shape=(
            state,
            state,
            state,
            jax.ShapeDtypeStruct((scen, flat), F32),
            iface_shape,
        ),
        in_specs=[hbm] * 10,
        out_specs=(hbm,) * 5,
        scratch_shapes=[
            pltpu.VMEM(volt_init.shape, F32),
            pltpu.VMEM(volt_init.shape, F32),
            pltpu.VMEM(local_inverse.shape, BF16),
            pltpu.VMEM(schur_inverse.shape, BF16),
            pltpu.VMEM(ind_gain.shape, F32),
            pltpu.VMEM(tie.shape, F32),
            pltpu.VMEM(port_map.shape, jnp.int32),
            pltpu.VMEM(breaker.shape, jnp.int32),
            pltpu.SMEM(fault_time.shape, jnp.int32),
            pltpu.SMEM(fault_node.shape, jnp.int32),
            pltpu.VMEM(volt_init.shape, F32),
            pltpu.VMEM((rows, sub, ports), jnp.int32),
            pltpu.VMEM((rows, cols * share, flat), BF16),
            pltpu.VMEM((rows, own_i, flat), BF16),
            pltpu.VMEM((STEPS, rows, 2 * scen, flat), BF16),
            pltpu.VMEM((STEPS, cols, scen, share), BF16),
            pltpu.VMEM((STEPS, rows * cols, scen, share), BF16),
            pltpu.VMEM((STEPS, PIECES, cols, scen, own_i // PIECES), BF16),
            pltpu.VMEM((STEPS, PIECES, cols, scen, own_i // PIECES), BF16),
            pltpu.VMEM((STEPS, rows, 2 * scen, flat), BF16),
            pltpu.VMEM((STEPS, rows, 2 * scen, flat), BF16),
            pltpu.VMEM((scen, flat), F32),
            pltpu.VMEM((scen, own_i), F32),
            pltpu.SemaphoreType.DMA((10,)),
            pltpu.SemaphoreType.DMA((5,)),
            pltpu.SemaphoreType.DMA((1 + (3 + PIECES) * STEPS,)),
            pltpu.SemaphoreType.DMA((1 + (3 + PIECES) * STEPS,)),
            pltpu.SemaphoreType.DMA((STEPS, rows - 1)),
        ],
        compiler_params=pltpu.CompilerParams(
            collective_id=0, has_side_effects=True, vmem_limit_bytes=60 * 1024 * 1024
        ),
    )(
        volt_init,
        curr_init,
        local_inverse,
        schur_inverse,
        ind_gain,
        tie,
        port_map,
        breaker,
        fault_time,
        fault_node,
    )
    return pl.pallas_call(
        update_kernel,
        out_shape=(state, state, iface_shape),
        in_specs=[hbm] * 9,
        out_specs=(vmem, vmem, vmem),
        scratch_shapes=[
            pltpu.VMEM(volt_init.shape, F32),
            pltpu.VMEM(volt_init.shape, F32),
            pltpu.VMEM(volt_init.shape, F32),
            pltpu.VMEM((sub, ports, nodes), BF16),
            pltpu.VMEM(ind_gain.shape, F32),
            pltpu.VMEM(tie.shape, F32),
            pltpu.VMEM(breaker.shape, jnp.int32),
            pltpu.VMEM((scen, flat), F32),
            pltpu.SemaphoreType.DMA((9,)),
        ],
        compiler_params=pltpu.CompilerParams(vmem_limit_bytes=60 * 1024 * 1024),
    )(volt, curr, open_volt, local_inverse, ind_gain, tie, breaker, picked, iface)


def plain(
    volt_init,
    curr_init,
    local_inverse,
    schur_inverse,
    ind_gain,
    tie,
    port_map,
    breaker,
    fault_time,
    fault_node,
):
    sub_count, scen_count, node_count = volt_init.shape
    port_count = tie.shape[1]
    iface_width = lax.axis_size("row") * schur_inverse.shape[0]
    volt = volt_init
    curr = curr_init
    closed = breaker.astype(F32)
    first_sub = lax.axis_index("row") * sub_count
    node_ids = (first_sub + jnp.arange(sub_count, dtype=jnp.int32))[
        :, None
    ] * node_count + jnp.arange(node_count, dtype=jnp.int32)[None, :]
    hits = node_ids[:, None, :] == fault_node[None, :, None]
    flat_map = port_map.reshape(-1)
    port_inverse = local_inverse[:, :port_count, :]
    iface_block = jnp.zeros((scen_count, schur_inverse.shape[0]), F32)
    for step in range(STEPS):
        hist = closed * (curr + ind_gain[:, None, :] * volt)
        active = (step >= fault_time)[None, :, None]
        fault_on = jnp.where(hits & active, 1.0, 0.0).astype(F32)
        inject = (-hist - 2.0 * fault_on * volt).astype(BF16)
        open_volt = jnp.einsum("ksn,knm->ksm", inject, local_inverse, preferred_element_type=F32)
        values = tie[:, None, :] * open_volt[:, :, :port_count]
        flat_values = jnp.transpose(values, (0, 2, 1)).reshape(sub_count * port_count, scen_count)
        partial_rhs = jax.ops.segment_sum(flat_values, flat_map, iface_width).T
        owned = lax.psum_scatter(partial_rhs, "row", scatter_dimension=1, tiled=True)
        rhs_half = lax.all_gather(owned.astype(BF16), "row", axis=1, tiled=True)
        iface_block = dot_nt(rhs_half, lax.all_gather(schur_inverse, "col", axis=1, tiled=True))
        iface_full = lax.all_gather(iface_block, "row", axis=1, tiled=True)
        picked = jnp.take(iface_full, flat_map, axis=1).reshape(scen_count, sub_count, port_count)
        drive = (tie[:, None, :] * jnp.transpose(picked, (1, 0, 2))).astype(BF16)
        volt_next = open_volt + jnp.einsum(
            "ksp,kpn->ksn", drive, port_inverse, preferred_element_type=F32
        )
        curr = closed * (curr + ind_gain[:, None, :] * (volt_next + volt))
        volt = volt_next
    return (volt, curr, iface_block)


def local(*args):
    volt_init, schur_inverse, tie = args[0], args[3], args[5]
    sub, scen, _ = volt_init.shape
    own_i, own_j = schur_inverse.shape
    aligned = (
        own_j % (lax.axis_size("row") * LANES) == 0
        and own_i % (PIECES * LANES) == 0
        and scen % 16 == 0
        and sub % 2 == 0
        and 2 * tie.shape[1] == LANES
    )
    return fused(*args) if aligned else plain(*args)


def solution(mesh):
    placed = (
        P("row", "col", None),
        P("row", "col", None),
        P("row", None, None),
        P("row", "col"),
        P("row", None),
        P("row", None),
        P("row", None),
        P("row", "col", None),
        P("col"),
        P("col"),
    )
    return jax.shard_map(
        local,
        mesh=mesh,
        in_specs=placed,
        out_specs=(P("row", "col", None), P("row", "col", None), P("col", "row")),
        check_vma=False,
    )
```

```python
import functools

import jax
import jax.numpy as jnp
from jax import lax
from jax.experimental import pallas as pl
from jax.experimental.pallas import tpu as pltpu
from jax.sharding import PartitionSpec as P

STEPS = 2
PIECES = 2
LANES = 128
MESH = pl.DeviceIdType.MESH
F32 = jnp.float32
BF16 = jnp.bfloat16


def halves(x):
    high = x.astype(BF16)
    low = (x - high.astype(F32)).astype(BF16)
    return jnp.concatenate([high, low], axis=0)


def joined(x, count):
    return x[:count].astype(F32) + x[count:].astype(F32)


def dot_nt(a, b):
    return lax.dot_general(a, b, (((1,), (1,)), ((), ())), preferred_element_type=F32)


def dot_nn(a, b):
    return lax.dot_general(a, b, (((1,), (0,)), ((), ())), preferred_element_type=F32)


def kernel(
    rows,
    cols,
    volt_hbm,
    curr_hbm,
    linv_hbm,
    schur_hbm,
    gain_hbm,
    tie_hbm,
    map_hbm,
    breaker_hbm,
    time_hbm,
    node_hbm,
    volt_out,
    curr_out,
    open_out,
    picked_out,
    iface_out,
    volt_ref,
    curr_ref,
    linv,
    schur,
    turned,
    gain_ref,
    tie_ref,
    map_ref,
    breaker_ref,
    time_ref,
    node_ref,
    open_volt,
    map_in,
    spread,
    pick,
    val_in,
    rhs_send,
    rhs_in,
    part_send,
    part_in,
    pick_send,
    pick_in,
    picked_ref,
    iface_ref,
    load_sem,
    store_sem,
    send_sem,
    recv_sem,
    val_sem,
):
    sub, scen, nodes = volt_ref.shape
    ports = tie_ref.shape[1]
    half = sub // 2
    own_i, own_j = schur.shape
    share = own_j // rows
    piece = own_i // PIECES
    r = lax.axis_index("row")
    c = lax.axis_index("col")
    others = rows * cols - 1

    loads = [
        pltpu.make_async_copy(src, dst, load_sem.at[n])
        for n, (src, dst) in enumerate(
            (
                (time_hbm, time_ref),
                (node_hbm, node_ref),
                (gain_hbm, gain_ref),
                (tie_hbm, tie_ref),
                (map_hbm, map_ref),
                (volt_hbm, volt_ref),
                (curr_hbm, curr_ref),
                (breaker_hbm, breaker_ref),
                (linv_hbm, linv),
                (schur_hbm, schur),
            )
        )
    ]
    for load in loads:
        load.start()

    barrier = pltpu.get_barrier_semaphore()

    def greet(t, _):
        there = (lax.rem(r + t // cols, rows), lax.rem(c + lax.rem(t, cols), cols))
        pl.semaphore_signal(barrier, inc=1, device_id=there, device_id_type=MESH)
        return 0

    lax.fori_loop(1, rows * cols, greet, 0)
    for load in loads[:-1]:
        load.wait()

    def wait_bytes(ref, sem):
        pltpu.make_async_copy(ref, ref, sem).wait()

    def send(src, dst, phase, there, recv=None):
        pltpu.make_async_remote_copy(
            src_ref=src,
            dst_ref=dst,
            send_sem=send_sem.at[phase],
            recv_sem=recv_sem.at[phase] if recv is None else recv,
            device_id=there,
            device_id_type=MESH,
        ).start()

    def row_peer(d):
        return lax.rem(r + d, rows)

    far_first = sorted(range(1, rows), key=lambda d: abs(d - rows // 2))

    scen_ids = lax.broadcasted_iota(jnp.int32, (scen, 1), 0)
    f_node = jnp.zeros((scen, 1), jnp.int32)
    f_time = jnp.zeros((scen, 1), jnp.int32)
    for s in range(scen):
        f_node = jnp.where(scen_ids == s, node_ref[s], f_node)
        f_time = jnp.where(scen_ids == s, time_ref[s], f_time)
    node_ids = lax.broadcasted_iota(jnp.int32, (scen, nodes), 1)

    def injection(step, k, volt, curr):
        closed = breaker_ref[k].astype(F32)
        hist = closed * (curr + gain_ref[k : k + 1, :] * volt)
        here = f_node - (r * sub + k) * nodes
        on = jnp.logical_and(node_ids == here, f_time <= step)
        fault_on = jnp.where(on, 1.0, 0.0).astype(F32)
        return (-hist - 2.0 * fault_on * volt).astype(BF16)

    ids = lax.broadcasted_iota(jnp.int32, (LANES, LANES), 0).astype(F32).astype(BF16)
    lane_ids = lax.broadcasted_iota(jnp.int32, (1, LANES), 1)
    one = jnp.ones((LANES, LANES), BF16)
    zero = jnp.zeros((LANES, LANES), BF16)

    def hits(m):
        near = jnp.clip(m, -1, LANES).astype(F32).astype(BF16)
        return jnp.where(ids == near, one, zero)

    def packed_map(m, g):
        return jnp.concatenate([m[g : g + 1], m[g + half : g + half + 1]], axis=1)

    def fill_spread(q, maps):
        for g in range(half):
            m = packed_map(maps, g).astype(F32)
            down = jnp.broadcast_to(m, (LANES, LANES)).T
            for b in range(cols):
                for e in range(share // LANES):
                    first = b * share + e * LANES
                    across = lane_ids + (b * own_j + r * share + e * LANES)
                    spread[q, g * LANES : (g + 1) * LANES, first : first + LANES] = jnp.where(
                        down == across.astype(F32), 1.0, 0.0
                    ).astype(BF16)

    def fill_pick(q, maps):
        for g in range(half):
            m = packed_map(maps, g) - r * own_i
            for e in range(own_i // LANES):
                pick[q, e * LANES : (e + 1) * LANES, g * LANES : (g + 1) * LANES] = hits(
                    m - e * LANES
                )

    stores = []

    def store(src, dst):
        copy = pltpu.make_async_copy(src, dst, store_sem.at[len(stores)])
        copy.start()
        stores.append(copy)

    for step in range(STEPS):
        base = 1 + (3 + PIECES) * step
        last = step == STEPS - 1
        injects = [injection(step, k, volt_ref[k], curr_ref[k]) for k in range(sub)]
        for k in range(sub):
            open_volt[k] = dot_nn(injects[k], linv[k])

        def port_values(k):
            return tie_ref[k : k + 1, :] * open_volt[k, :, :ports]

        vals = jnp.concatenate(
            [
                jnp.concatenate([port_values(g), port_values(g + half)], axis=1)
                for g in range(half)
            ],
            axis=1,
        )
        val_in[step, r] = halves(vals)
        if last:
            store(volt_ref, volt_out)
            store(curr_ref, curr_out)
            store(open_volt, open_out)
        if step == 0:
            pl.semaphore_wait(barrier, others)
            for d in far_first:
                send(map_ref, map_in.at[r], 0, (row_peer(d), c))
        for d in far_first:
            mine = val_in.at[step, r]
            send(mine, mine, base, (row_peer(d), c), val_sem.at[step, d - 1])

        if step == 0:
            fill_spread(r, map_ref[...])
            fill_pick(r, map_ref[...])
            wait_bytes(map_in.at[pl.ds(0, rows - 1)], recv_sem.at[0])

            def fill_rest(d, _):
                fill_spread(row_peer(d), map_in[row_peer(d)])
                return 0

            lax.fori_loop(1, rows, fill_rest, 0)

        rhs = dot_nn(val_in[step, r], spread[r])
        for d in reversed(far_first):
            q = row_peer(rows - d)
            wait_bytes(val_in.at[step, q], val_sem.at[step, d - 1])
            rhs += dot_nn(val_in[step, q], spread[q])
        rhs = joined(rhs, scen).astype(BF16)
        for b in range(cols):
            rhs_send[step, b] = rhs[:, b * share : (b + 1) * share]

        def send_rhs(t, _):
            peer_r = lax.rem(r + t // cols, rows)
            peer_c = lax.rem(c + lax.rem(t, cols), cols)
            send(
                rhs_send.at[step, peer_c],
                rhs_in.at[step, r * cols + c],
                base + 1,
                (peer_r, peer_c),
            )
            return 0

        lax.fori_loop(1, rows * cols, send_rhs, 0)
        rhs_in[step, r * cols + c] = rhs_send[step, c]

        if step == 0:

            def fill_rest_pick(d, _):
                fill_pick(row_peer(d), map_in[row_peer(d)])
                return 0

            lax.fori_loop(1, rows, fill_rest_pick, 0)
            loads[-1].wait()
            turned[...] = schur[...].T

        wait_bytes(rhs_in.at[step, pl.ds(0, others)], recv_sem.at[base + 1])
        wide = jnp.concatenate(
            [
                rhs_in[step, q * cols : (q + 1) * cols].reshape(cols * scen, share)
                for q in range(rows)
            ],
            axis=1,
        )
        for h in range(PIECES):
            part = dot_nn(wide, turned[:, h * piece : (h + 1) * piece]).astype(BF16)
            part_send[step, h] = part.reshape(cols, scen, piece)
            for d in range(1, cols):
                peer = lax.rem(c + d, cols)
                send(
                    part_send.at[step, h, peer],
                    part_in.at[step, h, c],
                    base + 2 + h,
                    (r, peer),
                )
            part_in[step, h, c] = part_send[step, h, c]

        def summed(h):
            wait_bytes(part_in.at[step, h, pl.ds(0, cols - 1)], recv_sem.at[base + 2 + h])
            iface = part_in[step, h, 0].astype(F32)
            for b in range(1, cols):
                iface += part_in[step, h, b].astype(F32)
            if last:
                iface_ref[:, h * piece : (h + 1) * piece] = iface
            return halves(iface)

        order = far_first + [0]
        totals = {}
        for h in range(PIECES):
            iface = summed(h)
            for d in order:
                q = row_peer(d)
                term = dot_nn(iface, pick[q, h * piece : (h + 1) * piece, :])
                totals[d] = term if h == 0 else totals[d] + term
                if h == PIECES - 1:
                    if d == 0:
                        pick_in[step, r] = totals[d].astype(BF16)
                    else:
                        pick_send[step, q] = totals[d].astype(BF16)
                        send(
                            pick_send.at[step, q],
                            pick_in.at[step, r],
                            base + 2 + PIECES,
                            (q, c),
                        )
        if last:
            store(iface_ref, iface_out)
        wait_bytes(pick_in.at[step, pl.ds(0, rows - 1)], recv_sem.at[base + 2 + PIECES])
        picked = joined(pick_in[step, 0], scen)
        for q in range(1, rows):
            picked += joined(pick_in[step, q], scen)

        if last:
            picked_ref[...] = picked
            store(picked_ref, picked_out)
            break
        drives = []
        for k in range(sub):
            first = (k % half) * LANES + (k // half) * ports
            drives.append((tie_ref[k : k + 1, :] * picked[:, first : first + ports]).astype(BF16))
        for k in range(sub):
            volt, curr = volt_ref[k], curr_ref[k]
            volt_next = open_volt[k] + dot_nn(drives[k], linv[k, :ports, :])
            closed = breaker_ref[k].astype(F32)
            curr_ref[k] = closed * (curr + gain_ref[k : k + 1, :] * (volt_next + volt))
            volt_ref[k] = volt_next

    for copy in stores:
        copy.wait()
    wait_bytes(map_in.at[pl.ds(0, rows - 1)], send_sem.at[0])
    for step in range(STEPS):
        base = 1 + (3 + PIECES) * step
        wait_bytes(val_in.at[step, pl.ds(0, rows - 1)], send_sem.at[base])
        wait_bytes(rhs_in.at[step, pl.ds(0, others)], send_sem.at[base + 1])
        for h in range(PIECES):
            wait_bytes(part_in.at[step, h, pl.ds(0, cols - 1)], send_sem.at[base + 2 + h])
        wait_bytes(pick_in.at[step, pl.ds(0, rows - 1)], send_sem.at[base + 2 + PIECES])


def update_kernel(
    volt_hbm,
    curr_hbm,
    open_hbm,
    linv_hbm,
    gain_hbm,
    tie_hbm,
    breaker_hbm,
    picked_hbm,
    iface_hbm,
    volt_out,
    curr_out,
    iface_out,
    volt_ref,
    curr_ref,
    open_ref,
    linv,
    gain_ref,
    tie_ref,
    breaker_ref,
    picked_ref,
    load_sem,
):
    sub = volt_ref.shape[0]
    ports = tie_ref.shape[1]
    half = sub // 2
    pairs = (
        (linv_hbm.at[:, pl.ds(0, ports), :], linv),
        (picked_hbm, picked_ref),
        (tie_hbm, tie_ref),
        (gain_hbm, gain_ref),
        (open_hbm, open_ref),
        (volt_hbm, volt_ref),
        (curr_hbm, curr_ref),
        (breaker_hbm, breaker_ref),
        (iface_hbm, iface_out),
    )
    loads = [
        pltpu.make_async_copy(src, dst, load_sem.at[n]) for n, (src, dst) in enumerate(pairs)
    ]
    for load in loads:
        load.start()
    for load in loads:
        load.wait()
    for k in range(sub):
        first = (k % half) * LANES + (k // half) * ports
        drive = (tie_ref[k : k + 1, :] * picked_ref[:, first : first + ports]).astype(BF16)
        volt_next = open_ref[k] + dot_nn(drive, linv[k])
        closed = breaker_ref[k].astype(F32)
        curr_out[k] = closed * (curr_ref[k] + gain_ref[k : k + 1, :] * (volt_next + volt_ref[k]))
        volt_out[k] = volt_next


def fused(
    volt_init,
    curr_init,
    local_inverse,
    schur_inverse,
    ind_gain,
    tie,
    port_map,
    breaker,
    fault_time,
    fault_node,
):
    rows, cols = lax.axis_size("row"), lax.axis_size("col")
    sub, scen, nodes = volt_init.shape
    ports = tie.shape[1]
    own_i, own_j = schur_inverse.shape
    share = own_j // rows
    flat = sub * ports
    vmem = pl.BlockSpec(memory_space=pltpu.VMEM)
    hbm = pl.BlockSpec(memory_space=pltpu.HBM)
    state = jax.ShapeDtypeStruct(volt_init.shape, F32)
    iface_shape = jax.ShapeDtypeStruct((scen, own_i), F32)
    volt, curr, open_volt, picked, iface = pl.pallas_call(
        functools.partial(kernel, rows, cols),
        out_shape=(
            state,
            state,
            state,
            jax.ShapeDtypeStruct((scen, flat), F32),
            iface_shape,
        ),
        in_specs=[hbm] * 10,
        out_specs=(hbm,) * 5,
        scratch_shapes=[
            pltpu.VMEM(volt_init.shape, F32),
            pltpu.VMEM(volt_init.shape, F32),
            pltpu.VMEM(local_inverse.shape, BF16),
            pltpu.VMEM(schur_inverse.shape, BF16),
            pltpu.VMEM((own_j, own_i), BF16),
            pltpu.VMEM(ind_gain.shape, F32),
            pltpu.VMEM(tie.shape, F32),
            pltpu.VMEM(port_map.shape, jnp.int32),
            pltpu.VMEM(breaker.shape, jnp.int32),
            pltpu.SMEM(fault_time.shape, jnp.int32),
            pltpu.SMEM(fault_node.shape, jnp.int32),
            pltpu.VMEM(volt_init.shape, F32),
            pltpu.VMEM((rows, sub, ports), jnp.int32),
            pltpu.VMEM((rows, flat, cols * share), BF16),
            pltpu.VMEM((rows, own_i, flat), BF16),
            pltpu.VMEM((STEPS, rows, 2 * scen, flat), BF16),
            pltpu.VMEM((STEPS, cols, scen, share), BF16),
            pltpu.VMEM((STEPS, rows * cols, scen, share), BF16),
            pltpu.VMEM((STEPS, PIECES, cols, scen, own_i // PIECES), BF16),
            pltpu.VMEM((STEPS, PIECES, cols, scen, own_i // PIECES), BF16),
            pltpu.VMEM((STEPS, rows, 2 * scen, flat), BF16),
            pltpu.VMEM((STEPS, rows, 2 * scen, flat), BF16),
            pltpu.VMEM((scen, flat), F32),
            pltpu.VMEM((scen, own_i), F32),
            pltpu.SemaphoreType.DMA((10,)),
            pltpu.SemaphoreType.DMA((5,)),
            pltpu.SemaphoreType.DMA((1 + (3 + PIECES) * STEPS,)),
            pltpu.SemaphoreType.DMA((1 + (3 + PIECES) * STEPS,)),
            pltpu.SemaphoreType.DMA((STEPS, rows - 1)),
        ],
        compiler_params=pltpu.CompilerParams(
            collective_id=0, has_side_effects=True, vmem_limit_bytes=60 * 1024 * 1024
        ),
    )(
        volt_init,
        curr_init,
        local_inverse,
        schur_inverse,
        ind_gain,
        tie,
        port_map,
        breaker,
        fault_time,
        fault_node,
    )
    return pl.pallas_call(
        update_kernel,
        out_shape=(state, state, iface_shape),
        in_specs=[hbm] * 9,
        out_specs=(vmem, vmem, vmem),
        scratch_shapes=[
            pltpu.VMEM(volt_init.shape, F32),
            pltpu.VMEM(volt_init.shape, F32),
            pltpu.VMEM(volt_init.shape, F32),
            pltpu.VMEM((sub, ports, nodes), BF16),
            pltpu.VMEM(ind_gain.shape, F32),
            pltpu.VMEM(tie.shape, F32),
            pltpu.VMEM(breaker.shape, jnp.int32),
            pltpu.VMEM((scen, flat), F32),
            pltpu.SemaphoreType.DMA((9,)),
        ],
        compiler_params=pltpu.CompilerParams(vmem_limit_bytes=60 * 1024 * 1024),
    )(volt, curr, open_volt, local_inverse, ind_gain, tie, breaker, picked, iface)


def plain(
    volt_init,
    curr_init,
    local_inverse,
    schur_inverse,
    ind_gain,
    tie,
    port_map,
    breaker,
    fault_time,
    fault_node,
):
    sub_count, scen_count, node_count = volt_init.shape
    port_count = tie.shape[1]
    iface_width = lax.axis_size("row") * schur_inverse.shape[0]
    volt = volt_init
    curr = curr_init
    closed = breaker.astype(F32)
    first_sub = lax.axis_index("row") * sub_count
    node_ids = (first_sub + jnp.arange(sub_count, dtype=jnp.int32))[
        :, None
    ] * node_count + jnp.arange(node_count, dtype=jnp.int32)[None, :]
    hits = node_ids[:, None, :] == fault_node[None, :, None]
    flat_map = port_map.reshape(-1)
    port_inverse = local_inverse[:, :port_count, :]
    iface_block = jnp.zeros((scen_count, schur_inverse.shape[0]), F32)
    for step in range(STEPS):
        hist = closed * (curr + ind_gain[:, None, :] * volt)
        active = (step >= fault_time)[None, :, None]
        fault_on = jnp.where(hits & active, 1.0, 0.0).astype(F32)
        inject = (-hist - 2.0 * fault_on * volt).astype(BF16)
        open_volt = jnp.einsum("ksn,knm->ksm", inject, local_inverse, preferred_element_type=F32)
        values = tie[:, None, :] * open_volt[:, :, :port_count]
        flat_values = jnp.transpose(values, (0, 2, 1)).reshape(sub_count * port_count, scen_count)
        partial_rhs = jax.ops.segment_sum(flat_values, flat_map, iface_width).T
        owned = lax.psum_scatter(partial_rhs, "row", scatter_dimension=1, tiled=True)
        rhs_half = lax.all_gather(owned.astype(BF16), "row", axis=1, tiled=True)
        iface_block = dot_nt(rhs_half, lax.all_gather(schur_inverse, "col", axis=1, tiled=True))
        iface_full = lax.all_gather(iface_block, "row", axis=1, tiled=True)
        picked = jnp.take(iface_full, flat_map, axis=1).reshape(scen_count, sub_count, port_count)
        drive = (tie[:, None, :] * jnp.transpose(picked, (1, 0, 2))).astype(BF16)
        volt_next = open_volt + jnp.einsum(
            "ksp,kpn->ksn", drive, port_inverse, preferred_element_type=F32
        )
        curr = closed * (curr + ind_gain[:, None, :] * (volt_next + volt))
        volt = volt_next
    return (volt, curr, iface_block)


def local(*args):
    volt_init, schur_inverse, tie = args[0], args[3], args[5]
    sub, scen, _ = volt_init.shape
    own_i, own_j = schur_inverse.shape
    aligned = (
        own_j % (lax.axis_size("row") * LANES) == 0
        and own_i % (PIECES * LANES) == 0
        and scen % 16 == 0
        and sub % 2 == 0
        and 2 * tie.shape[1] == LANES
    )
    return fused(*args) if aligned else plain(*args)


def solution(mesh):
    placed = (
        P("row", "col", None),
        P("row", "col", None),
        P("row", None, None),
        P("row", "col"),
        P("row", None),
        P("row", None),
        P("row", None),
        P("row", "col", None),
        P("col"),
        P("col"),
    )
    return jax.shard_map(
        local,
        mesh=mesh,
        in_specs=placed,
        out_specs=(P("row", "col", None), P("row", "col", None), P("col", "row")),
        check_vma=False,
    )
```

```python
import functools

import jax
import jax.numpy as jnp
from jax import lax
from jax.experimental import pallas as pl
from jax.experimental.pallas import tpu as pltpu
from jax.sharding import PartitionSpec as P

STEPS = 2
PIECES = 1
LANES = 128
MESH = pl.DeviceIdType.MESH
F32 = jnp.float32
BF16 = jnp.bfloat16


def halves(x):
    high = x.astype(BF16)
    low = (x - high.astype(F32)).astype(BF16)
    return jnp.concatenate([high, low], axis=0)


def joined(x, count):
    return x[:count].astype(F32) + x[count:].astype(F32)


def dot_nt(a, b):
    return lax.dot_general(a, b, (((1,), (1,)), ((), ())), preferred_element_type=F32)


def dot_nn(a, b):
    return lax.dot_general(a, b, (((1,), (0,)), ((), ())), preferred_element_type=F32)


def kernel(
    rows,
    cols,
    volt_hbm,
    curr_hbm,
    linv_hbm,
    schur_hbm,
    gain_hbm,
    tie_hbm,
    map_hbm,
    breaker_hbm,
    time_hbm,
    node_hbm,
    volt_out,
    curr_out,
    open_out,
    picked_out,
    iface_out,
    volt_ref,
    curr_ref,
    linv,
    schur,
    turned,
    gain_ref,
    tie_ref,
    map_ref,
    breaker_ref,
    time_ref,
    node_ref,
    open_volt,
    map_in,
    spread,
    pick,
    val_in,
    rhs_send,
    rhs_in,
    part_send,
    part_in,
    pick_send,
    pick_in,
    picked_ref,
    iface_ref,
    load_sem,
    store_sem,
    send_sem,
    recv_sem,
    val_sem,
):
    sub, scen, nodes = volt_ref.shape
    ports = tie_ref.shape[1]
    half = sub // 2
    own_i, own_j = schur.shape
    share = own_j // rows
    piece = own_i // PIECES
    r = lax.axis_index("row")
    c = lax.axis_index("col")
    others = rows * cols - 1

    loads = [
        pltpu.make_async_copy(src, dst, load_sem.at[n])
        for n, (src, dst) in enumerate(
            (
                (time_hbm, time_ref),
                (node_hbm, node_ref),
                (gain_hbm, gain_ref),
                (tie_hbm, tie_ref),
                (map_hbm, map_ref),
                (volt_hbm, volt_ref),
                (curr_hbm, curr_ref),
                (breaker_hbm, breaker_ref),
                (linv_hbm, linv),
                (schur_hbm, schur),
            )
        )
    ]
    for load in loads:
        load.start()

    barrier = pltpu.get_barrier_semaphore()

    def greet(t, _):
        there = (lax.rem(r + t // cols, rows), lax.rem(c + lax.rem(t, cols), cols))
        pl.semaphore_signal(barrier, inc=1, device_id=there, device_id_type=MESH)
        return 0

    lax.fori_loop(1, rows * cols, greet, 0)
    for load in loads[:-1]:
        load.wait()

    def wait_bytes(ref, sem):
        pltpu.make_async_copy(ref, ref, sem).wait()

    def send(src, dst, phase, there, recv=None):
        pltpu.make_async_remote_copy(
            src_ref=src,
            dst_ref=dst,
            send_sem=send_sem.at[phase],
            recv_sem=recv_sem.at[phase] if recv is None else recv,
            device_id=there,
            device_id_type=MESH,
        ).start()

    def row_peer(d):
        return lax.rem(r + d, rows)

    far_first = sorted(range(1, rows), key=lambda d: abs(d - rows // 2))

    scen_ids = lax.broadcasted_iota(jnp.int32, (scen, 1), 0)
    f_node = jnp.zeros((scen, 1), jnp.int32)
    f_time = jnp.zeros((scen, 1), jnp.int32)
    for s in range(scen):
        f_node = jnp.where(scen_ids == s, node_ref[s], f_node)
        f_time = jnp.where(scen_ids == s, time_ref[s], f_time)
    node_ids = lax.broadcasted_iota(jnp.int32, (scen, nodes), 1)

    def injection(step, k, volt, curr):
        closed = breaker_ref[k].astype(F32)
        hist = closed * (curr + gain_ref[k : k + 1, :] * volt)
        here = f_node - (r * sub + k) * nodes
        on = jnp.logical_and(node_ids == here, f_time <= step)
        fault_on = jnp.where(on, 1.0, 0.0).astype(F32)
        return (-hist - 2.0 * fault_on * volt).astype(BF16)

    ids = lax.broadcasted_iota(jnp.int32, (LANES, LANES), 0).astype(F32).astype(BF16)
    lane_ids = lax.broadcasted_iota(jnp.int32, (1, LANES), 1)
    one = jnp.ones((LANES, LANES), BF16)
    zero = jnp.zeros((LANES, LANES), BF16)

    def hits(m):
        near = jnp.clip(m, -1, LANES).astype(F32).astype(BF16)
        return jnp.where(ids == near, one, zero)

    def packed_map(m, g):
        return jnp.concatenate([m[g : g + 1], m[g + half : g + half + 1]], axis=1)

    def fill_spread(q, maps):
        for g in range(half):
            m = packed_map(maps, g).astype(F32)
            down = jnp.broadcast_to(m, (LANES, LANES)).T
            for b in range(cols):
                for e in range(share // LANES):
                    first = b * share + e * LANES
                    across = lane_ids + (b * own_j + r * share + e * LANES)
                    spread[q, g * LANES : (g + 1) * LANES, first : first + LANES] = jnp.where(
                        down == across.astype(F32), 1.0, 0.0
                    ).astype(BF16)

    def fill_pick(q, maps):
        for g in range(half):
            m = packed_map(maps, g) - r * own_i
            for e in range(own_i // LANES):
                pick[q, e * LANES : (e + 1) * LANES, g * LANES : (g + 1) * LANES] = hits(
                    m - e * LANES
                )

    stores = []

    def store(src, dst):
        copy = pltpu.make_async_copy(src, dst, store_sem.at[len(stores)])
        copy.start()
        stores.append(copy)

    for step in range(STEPS):
        base = 1 + (3 + PIECES) * step
        last = step == STEPS - 1
        injects = [injection(step, k, volt_ref[k], curr_ref[k]) for k in range(sub)]
        for k in range(sub):
            open_volt[k] = dot_nn(injects[k], linv[k])

        def port_values(k):
            return tie_ref[k : k + 1, :] * open_volt[k, :, :ports]

        vals = jnp.concatenate(
            [
                jnp.concatenate([port_values(g), port_values(g + half)], axis=1)
                for g in range(half)
            ],
            axis=1,
        )
        val_in[step, r] = halves(vals)
        if last:
            store(volt_ref, volt_out)
            store(curr_ref, curr_out)
            store(open_volt, open_out)
        if step == 0:
            pl.semaphore_wait(barrier, others)
            for d in far_first:
                send(map_ref, map_in.at[r], 0, (row_peer(d), c))
        for d in far_first:
            mine = val_in.at[step, r]
            send(mine, mine, base, (row_peer(d), c), val_sem.at[step, d - 1])

        if step == 0:
            fill_spread(r, map_ref[...])
            fill_pick(r, map_ref[...])
            wait_bytes(map_in.at[pl.ds(0, rows - 1)], recv_sem.at[0])

            def fill_rest(d, _):
                fill_spread(row_peer(d), map_in[row_peer(d)])
                return 0

            lax.fori_loop(1, rows, fill_rest, 0)

        rhs = dot_nn(val_in[step, r], spread[r])
        for d in reversed(far_first):
            q = row_peer(rows - d)
            wait_bytes(val_in.at[step, q], val_sem.at[step, d - 1])
            rhs += dot_nn(val_in[step, q], spread[q])
        rhs = joined(rhs, scen).astype(BF16)
        for b in range(cols):
            rhs_send[step, b] = rhs[:, b * share : (b + 1) * share]

        def send_rhs(t, _):
            peer_r = lax.rem(r + t // cols, rows)
            peer_c = lax.rem(c + lax.rem(t, cols), cols)
            send(
                rhs_send.at[step, peer_c],
                rhs_in.at[step, r * cols + c],
                base + 1,
                (peer_r, peer_c),
            )
            return 0

        lax.fori_loop(1, rows * cols, send_rhs, 0)
        rhs_in[step, r * cols + c] = rhs_send[step, c]

        if step == 0:

            def fill_rest_pick(d, _):
                fill_pick(row_peer(d), map_in[row_peer(d)])
                return 0

            lax.fori_loop(1, rows, fill_rest_pick, 0)
            loads[-1].wait()
            turned[...] = schur[...].T

        wait_bytes(rhs_in.at[step, pl.ds(0, others)], recv_sem.at[base + 1])
        wide = jnp.concatenate(
            [
                rhs_in[step, q * cols : (q + 1) * cols].reshape(cols * scen, share)
                for q in range(rows)
            ],
            axis=1,
        )
        for h in range(PIECES):
            part = dot_nn(wide, turned[:, h * piece : (h + 1) * piece]).astype(BF16)
            part_send[step, h] = part.reshape(cols, scen, piece)
            for d in range(1, cols):
                peer = lax.rem(c + d, cols)
                send(
                    part_send.at[step, h, peer],
                    part_in.at[step, h, c],
                    base + 2 + h,
                    (r, peer),
                )
            part_in[step, h, c] = part_send[step, h, c]

        def summed(h):
            wait_bytes(part_in.at[step, h, pl.ds(0, cols - 1)], recv_sem.at[base + 2 + h])
            iface = part_in[step, h, 0].astype(F32)
            for b in range(1, cols):
                iface += part_in[step, h, b].astype(F32)
            if last:
                iface_ref[:, h * piece : (h + 1) * piece] = iface
            return halves(iface)

        order = far_first + [0]
        totals = {}
        for h in range(PIECES):
            iface = summed(h)
            for d in order:
                q = row_peer(d)
                term = dot_nn(iface, pick[q, h * piece : (h + 1) * piece, :])
                totals[d] = term if h == 0 else totals[d] + term
                if h == PIECES - 1:
                    if d == 0:
                        pick_in[step, r] = totals[d].astype(BF16)
                    else:
                        pick_send[step, q] = totals[d].astype(BF16)
                        send(
                            pick_send.at[step, q],
                            pick_in.at[step, r],
                            base + 2 + PIECES,
                            (q, c),
                        )
        if last:
            store(iface_ref, iface_out)
        wait_bytes(pick_in.at[step, pl.ds(0, rows - 1)], recv_sem.at[base + 2 + PIECES])
        picked = joined(pick_in[step, 0], scen)
        for q in range(1, rows):
            picked += joined(pick_in[step, q], scen)

        if last:
            picked_ref[...] = picked
            store(picked_ref, picked_out)
            break
        drives = []
        for k in range(sub):
            first = (k % half) * LANES + (k // half) * ports
            drives.append((tie_ref[k : k + 1, :] * picked[:, first : first + ports]).astype(BF16))
        for k in range(sub):
            volt, curr = volt_ref[k], curr_ref[k]
            volt_next = open_volt[k] + dot_nn(drives[k], linv[k, :ports, :])
            closed = breaker_ref[k].astype(F32)
            curr_ref[k] = closed * (curr + gain_ref[k : k + 1, :] * (volt_next + volt))
            volt_ref[k] = volt_next

    for copy in stores:
        copy.wait()
    wait_bytes(map_in.at[pl.ds(0, rows - 1)], send_sem.at[0])
    for step in range(STEPS):
        base = 1 + (3 + PIECES) * step
        wait_bytes(val_in.at[step, pl.ds(0, rows - 1)], send_sem.at[base])
        wait_bytes(rhs_in.at[step, pl.ds(0, others)], send_sem.at[base + 1])
        for h in range(PIECES):
            wait_bytes(part_in.at[step, h, pl.ds(0, cols - 1)], send_sem.at[base + 2 + h])
        wait_bytes(pick_in.at[step, pl.ds(0, rows - 1)], send_sem.at[base + 2 + PIECES])


def update_kernel(
    volt_hbm,
    curr_hbm,
    open_hbm,
    linv_hbm,
    gain_hbm,
    tie_hbm,
    breaker_hbm,
    picked_hbm,
    iface_hbm,
    volt_out,
    curr_out,
    iface_out,
    volt_ref,
    curr_ref,
    open_ref,
    linv,
    gain_ref,
    tie_ref,
    breaker_ref,
    picked_ref,
    load_sem,
):
    sub = volt_ref.shape[0]
    ports = tie_ref.shape[1]
    half = sub // 2
    pairs = (
        (linv_hbm.at[:, pl.ds(0, ports), :], linv),
        (picked_hbm, picked_ref),
        (tie_hbm, tie_ref),
        (gain_hbm, gain_ref),
        (open_hbm, open_ref),
        (volt_hbm, volt_ref),
        (curr_hbm, curr_ref),
        (breaker_hbm, breaker_ref),
        (iface_hbm, iface_out),
    )
    loads = [
        pltpu.make_async_copy(src, dst, load_sem.at[n]) for n, (src, dst) in enumerate(pairs)
    ]
    for load in loads:
        load.start()
    for load in loads:
        load.wait()
    for k in range(sub):
        first = (k % half) * LANES + (k // half) * ports
        drive = (tie_ref[k : k + 1, :] * picked_ref[:, first : first + ports]).astype(BF16)
        volt_next = open_ref[k] + dot_nn(drive, linv[k])
        closed = breaker_ref[k].astype(F32)
        curr_out[k] = closed * (curr_ref[k] + gain_ref[k : k + 1, :] * (volt_next + volt_ref[k]))
        volt_out[k] = volt_next


def fused(
    volt_init,
    curr_init,
    local_inverse,
    schur_inverse,
    ind_gain,
    tie,
    port_map,
    breaker,
    fault_time,
    fault_node,
):
    rows, cols = lax.axis_size("row"), lax.axis_size("col")
    sub, scen, nodes = volt_init.shape
    ports = tie.shape[1]
    own_i, own_j = schur_inverse.shape
    share = own_j // rows
    flat = sub * ports
    vmem = pl.BlockSpec(memory_space=pltpu.VMEM)
    hbm = pl.BlockSpec(memory_space=pltpu.HBM)
    state = jax.ShapeDtypeStruct(volt_init.shape, F32)
    iface_shape = jax.ShapeDtypeStruct((scen, own_i), F32)
    volt, curr, open_volt, picked, iface = pl.pallas_call(
        functools.partial(kernel, rows, cols),
        out_shape=(
            state,
            state,
            state,
            jax.ShapeDtypeStruct((scen, flat), F32),
            iface_shape,
        ),
        in_specs=[hbm] * 10,
        out_specs=(hbm,) * 5,
        scratch_shapes=[
            pltpu.VMEM(volt_init.shape, F32),
            pltpu.VMEM(volt_init.shape, F32),
            pltpu.VMEM(local_inverse.shape, BF16),
            pltpu.VMEM(schur_inverse.shape, BF16),
            pltpu.VMEM((own_j, own_i), BF16),
            pltpu.VMEM(ind_gain.shape, F32),
            pltpu.VMEM(tie.shape, F32),
            pltpu.VMEM(port_map.shape, jnp.int32),
            pltpu.VMEM(breaker.shape, jnp.int32),
            pltpu.SMEM(fault_time.shape, jnp.int32),
            pltpu.SMEM(fault_node.shape, jnp.int32),
            pltpu.VMEM(volt_init.shape, F32),
            pltpu.VMEM((rows, sub, ports), jnp.int32),
            pltpu.VMEM((rows, flat, cols * share), BF16),
            pltpu.VMEM((rows, own_i, flat), BF16),
            pltpu.VMEM((STEPS, rows, 2 * scen, flat), BF16),
            pltpu.VMEM((STEPS, cols, scen, share), BF16),
            pltpu.VMEM((STEPS, rows * cols, scen, share), BF16),
            pltpu.VMEM((STEPS, PIECES, cols, scen, own_i // PIECES), BF16),
            pltpu.VMEM((STEPS, PIECES, cols, scen, own_i // PIECES), BF16),
            pltpu.VMEM((STEPS, rows, 2 * scen, flat), BF16),
            pltpu.VMEM((STEPS, rows, 2 * scen, flat), BF16),
            pltpu.VMEM((scen, flat), F32),
            pltpu.VMEM((scen, own_i), F32),
            pltpu.SemaphoreType.DMA((10,)),
            pltpu.SemaphoreType.DMA((5,)),
            pltpu.SemaphoreType.DMA((1 + (3 + PIECES) * STEPS,)),
            pltpu.SemaphoreType.DMA((1 + (3 + PIECES) * STEPS,)),
            pltpu.SemaphoreType.DMA((STEPS, rows - 1)),
        ],
        compiler_params=pltpu.CompilerParams(
            collective_id=0, has_side_effects=True, vmem_limit_bytes=60 * 1024 * 1024
        ),
    )(
        volt_init,
        curr_init,
        local_inverse,
        schur_inverse,
        ind_gain,
        tie,
        port_map,
        breaker,
        fault_time,
        fault_node,
    )
    return pl.pallas_call(
        update_kernel,
        out_shape=(state, state, iface_shape),
        in_specs=[hbm] * 9,
        out_specs=(vmem, vmem, vmem),
        scratch_shapes=[
            pltpu.VMEM(volt_init.shape, F32),
            pltpu.VMEM(volt_init.shape, F32),
            pltpu.VMEM(volt_init.shape, F32),
            pltpu.VMEM((sub, ports, nodes), BF16),
            pltpu.VMEM(ind_gain.shape, F32),
            pltpu.VMEM(tie.shape, F32),
            pltpu.VMEM(breaker.shape, jnp.int32),
            pltpu.VMEM((scen, flat), F32),
            pltpu.SemaphoreType.DMA((9,)),
        ],
        compiler_params=pltpu.CompilerParams(vmem_limit_bytes=60 * 1024 * 1024),
    )(volt, curr, open_volt, local_inverse, ind_gain, tie, breaker, picked, iface)


def plain(
    volt_init,
    curr_init,
    local_inverse,
    schur_inverse,
    ind_gain,
    tie,
    port_map,
    breaker,
    fault_time,
    fault_node,
):
    sub_count, scen_count, node_count = volt_init.shape
    port_count = tie.shape[1]
    iface_width = lax.axis_size("row") * schur_inverse.shape[0]
    volt = volt_init
    curr = curr_init
    closed = breaker.astype(F32)
    first_sub = lax.axis_index("row") * sub_count
    node_ids = (first_sub + jnp.arange(sub_count, dtype=jnp.int32))[
        :, None
    ] * node_count + jnp.arange(node_count, dtype=jnp.int32)[None, :]
    hits = node_ids[:, None, :] == fault_node[None, :, None]
    flat_map = port_map.reshape(-1)
    port_inverse = local_inverse[:, :port_count, :]
    iface_block = jnp.zeros((scen_count, schur_inverse.shape[0]), F32)
    for step in range(STEPS):
        hist = closed * (curr + ind_gain[:, None, :] * volt)
        active = (step >= fault_time)[None, :, None]
        fault_on = jnp.where(hits & active, 1.0, 0.0).astype(F32)
        inject = (-hist - 2.0 * fault_on * volt).astype(BF16)
        open_volt = jnp.einsum("ksn,knm->ksm", inject, local_inverse, preferred_element_type=F32)
        values = tie[:, None, :] * open_volt[:, :, :port_count]
        flat_values = jnp.transpose(values, (0, 2, 1)).reshape(sub_count * port_count, scen_count)
        partial_rhs = jax.ops.segment_sum(flat_values, flat_map, iface_width).T
        owned = lax.psum_scatter(partial_rhs, "row", scatter_dimension=1, tiled=True)
        rhs_half = lax.all_gather(owned.astype(BF16), "row", axis=1, tiled=True)
        iface_block = dot_nt(rhs_half, lax.all_gather(schur_inverse, "col", axis=1, tiled=True))
        iface_full = lax.all_gather(iface_block, "row", axis=1, tiled=True)
        picked = jnp.take(iface_full, flat_map, axis=1).reshape(scen_count, sub_count, port_count)
        drive = (tie[:, None, :] * jnp.transpose(picked, (1, 0, 2))).astype(BF16)
        volt_next = open_volt + jnp.einsum(
            "ksp,kpn->ksn", drive, port_inverse, preferred_element_type=F32
        )
        curr = closed * (curr + ind_gain[:, None, :] * (volt_next + volt))
        volt = volt_next
    return (volt, curr, iface_block)


def local(*args):
    volt_init, schur_inverse, tie = args[0], args[3], args[5]
    sub, scen, _ = volt_init.shape
    own_i, own_j = schur_inverse.shape
    aligned = (
        own_j % (lax.axis_size("row") * LANES) == 0
        and own_i % (PIECES * LANES) == 0
        and scen % 16 == 0
        and sub % 2 == 0
        and 2 * tie.shape[1] == LANES
    )
    return fused(*args) if aligned else plain(*args)


def solution(mesh):
    placed = (
        P("row", "col", None),
        P("row", "col", None),
        P("row", None, None),
        P("row", "col"),
        P("row", None),
        P("row", None),
        P("row", None),
        P("row", "col", None),
        P("col"),
        P("col"),
    )
    return jax.shard_map(
        local,
        mesh=mesh,
        in_specs=placed,
        out_specs=(P("row", "col", None), P("row", "col", None), P("col", "row")),
        check_vma=False,
    )
```
